256 devices in a mesh: ch: 64 (over z, y, core), sp: 4 (over x).
Axes of the slice: x: 4, y: 4, z: 8, core: 2. Of those that a mesh axis runs over, the one named last changes fastest.
Arguments:
- volume: bfloat16 [256, 20, 64, 128], P('ch', 'sp'), may hold values from -6 to 6
- weight: bfloat16 [256, 27, 256], P('ch'), may hold values from -0.078125 to 0.078125
- channel_bias: bfloat16 [256], P('ch'), may hold values from -3 to 3
Outputs:
- activated: bfloat16 [256, 20, 64, 128], P('ch', 'sp')
The draws below stay inside these ranges and needn't reach their ends.
All inputs are finite; a program needn't handle non-finite values.
Results may differ from the reference program's by a relative error of at most 0.0012.
Values may be sent and summed in bfloat16 or wider, within the bound.
A program may use at most 192 MiB of HBM per device.

```python
import jax
import jax.numpy as jnp
from jax import lax

CIN = 256
COUT = 256
NY = 64
NZ = 128
NX = 20


def block_levels(rng, shape, cuts, low, high):
    gain, own = 1.0, jax.random.fold_in(rng, 6)
    for position, shards_of in cuts:
        draws = jnp.exp(jax.random.uniform(jax.random.fold_in(own, position), (shards_of,), jnp.float32, low / len(cuts), high / len(cuts)))
        gain = gain * jnp.repeat(draws, shape[position] // shards_of).reshape([-1 if axis == position else 1 for axis in range(len(shape))])
    return gain


def normal_values(rng, dims, spread, most, pieces=(), kind=jnp.bfloat16):
    loudness = block_levels(rng, dims, pieces, -0.22, 0.18) if pieces else 1.0
    values = jax.random.normal(rng, dims, jnp.float32) * spread * loudness
    return jnp.minimum(jnp.maximum(values, -most), most).astype(kind)


def setup_inputs(seed: int = 0) -> dict:
    arg_keys = jax.random.split(jax.random.key(seed), 4)
    volume = normal_values(arg_keys[0], (CIN, NX, NY, NZ), 1.0, 6.0, ((0, 64), (1, 4)))
    weight = normal_values(arg_keys[1], (COUT, 27, CIN), (27 * CIN) ** -0.5, 0.078125, ((0, 64),))
    channel_bias = normal_values(arg_keys[2], (COUT,), 0.5, 3.0, ((0, 64),))
    return dict(volume=volume, weight=weight, channel_bias=channel_bias)


def reference(volume, weight, channel_bias):
    kernel = weight.astype(jnp.float32).reshape(COUT, 3, 3, 3, CIN).transpose(0, 4, 1, 2, 3)
    conv = lax.conv_general_dilated(volume.astype(jnp.float32)[None], kernel, (1, 1, 1), ((1, 1), (1, 1), (1, 1)), dimension_numbers=("NCDHW", "OIDHW", "NCDHW"), precision=lax.Precision.HIGHEST)[0]
    total = conv + channel_bias.astype(jnp.float32)[:, None, None, None]
    return jnp.where(total > 0, total, 0.3 * total).astype(jnp.bfloat16)
```

```python
import functools

import jax
import jax.numpy as jnp
from jax import lax
from jax.experimental import pallas as pl
from jax.experimental.pallas import tpu as pltpu
from jax.sharding import PartitionSpec as P

NYT = 4
NXT = 4
MESH = pl.DeviceIdType.MESH
F32 = jnp.float32
BF16 = jnp.bfloat16


def tap_slot(t):
    return t // 7 * 8 + t % 7 if t <= 20 else 24 + t - 20


def kernel(
    nz, v, w, b, out,
    fe, ed, rz, re, f, ge, g2, xz, X, ws, wz, wf, wt, O, oy, fo, oz,
    s_vz, r_vz, s_ed, r_ed, s_wz, r_wz, s_wy, r_wy, s_wx, r_wx,
    s_xy, r_xy, s_cc, r_cc, s_xh, r_xh, s_xf, r_xf, s_oy, r_oy, s_oz, r_oz, loc,
):
    blk = 4 * nz
    half = NYT * blk
    ch = lax.axis_index("ch")
    x = lax.axis_index("sp")
    c = lax.rem(ch, 2)
    y = lax.rem(lax.div(ch, 2), NYT)
    z = lax.div(ch, 2 * NYT)

    def at(zz, yy, cc, xx):
        return {"ch": (zz * NYT + yy) * 2 + cc, "sp": xx}

    def zk(k):
        return lax.rem(z + k + nz, nz)

    def yk(k):
        return lax.rem(y + k + NYT, NYT)

    xl, xr = lax.rem(x + NXT - 1, NXT), lax.rem(x + 1, NXT)
    sib = at(z, y, 1 - c, x)

    def send(src, dst, ss, rs, to):
        cp = pltpu.make_async_remote_copy(
            src_ref=src, dst_ref=dst, send_sem=ss, recv_sem=rs, device_id=to, device_id_type=MESH
        )
        cp.start()
        return cp

    def recv(dst, sem):
        pltpu.make_async_copy(dst, dst, sem).wait()

    def local(src, dst, sem):
        cp = pltpu.make_async_copy(src, dst, sem)
        cp.start()
        return cp

    sent = []

    bar = pltpu.get_barrier_semaphore()
    peers = [at(zk(k), y, c, x) for k in range(1, nz)]
    peers += [at(z, yk(k), c, x) for k in range(1, NYT)]
    peers += [sib, at(z, y, c, xl), at(z, y, c, xr)]
    for p in peers:
        pl.semaphore_signal(bar, inc=1, device_id=p, device_id_type=MESH)

    start = jnp.minimum(7 * x, 20)
    for i in range(7):
        ws[i] = w[start + i]
    bb = jnp.broadcast_to(b[...].astype(F32), (4, 4))
    eye = lax.broadcasted_iota(jnp.int32, (4, 4), 0) == lax.broadcasted_iota(jnp.int32, (4, 4), 1)
    col = jnp.sum(jnp.where(eye, bb, 0.0), axis=1, keepdims=True)
    ws[7] = jnp.broadcast_to(col, ws.shape[1:]).astype(BF16)

    for j in range(4):
        for p in range(5):
            base = (j * 5 + p) * nz * 8
            for k in range(nz):
                fe[base + 8 * k:base + 8 * k + 8, :] = v[j, p, k].astype(F32)
    zero_edge = jnp.zeros((20, 128), BF16)
    ed[0, 0] = zero_edge
    ed[nz - 1, 1] = zero_edge
    for k in range(1, nz):
        ed[k, 0] = fe[pl.ds(8 * k - 1, 20, stride=8 * nz), :].astype(BF16)
        ed[k - 1, 1] = fe[pl.ds(8 * k, 20, stride=8 * nz), :].astype(BF16)

    @pl.when(x == 0)
    def _():
        X[:, 0] = jnp.zeros_like(X[:, 0])

    @pl.when(x == NXT - 1)
    def _():
        X[:, 6] = jnp.zeros_like(X[:, 6])

    pl.semaphore_wait(bar, len(peers))

    for k in range(1, nz):
        sent.append(send(ws, wz.at[z], s_wz.at[k], r_wz.at[k], at(zk(k), y, c, x)))
    for k in range(1, nz):
        d = zk(k)
        sent.append(send(v.at[:, :, d], rz.at[z], s_vz.at[k], r_vz.at[k], at(d, y, c, x)))
        sent.append(send(ed.at[d], re.at[z], s_ed.at[k], r_ed.at[k], at(d, y, c, x)))
    own = [
        local(ws, wz.at[z], loc.at[0]),
        local(v.at[:, :, z], rz.at[z], loc.at[1]),
        local(ed.at[z], re.at[z], loc.at[2]),
    ]

    n_in = 2 * half
    i = lax.broadcasted_iota(jnp.int32, (n_in, n_in), 0)
    o = lax.broadcasted_iota(jnp.int32, (n_in, n_in), 1)
    to = ((i >> 2) & 1) * half + ((i >> 3) & 3) * blk + (i >> 5) * 4 + (i & 3)
    perm = jnp.where(to == o, 1.0, 0.0).astype(BF16)

    own[0].wait()
    for k in range(1, nz):
        recv(wz.at[zk(-k)], r_wz.at[k])
    for t in range(8):
        for s in range(nz):
            wf[t, 4 * s:4 * s + 4, :] = wz[s, t].astype(F32)
    yoff = pl.multiple_of(y * blk, blk)
    for t in range(8):
        wt[8 * x + t, pl.ds(yoff, blk), :] = jnp.dot(
            wf[t].astype(BF16), perm, preferred_element_type=F32
        ).astype(BF16)
    mine = wt.at[pl.ds(8 * x, 8), pl.ds(yoff, blk), :]
    for k in range(1, NYT):
        sent.append(send(mine, mine, s_wy.at[k], r_wy.at[k], at(z, yk(k), c, x)))

    own[1].wait()
    own[2].wait()
    for k in range(1, nz):
        recv(rz.at[zk(-k)], r_vz.at[k])
        recv(re.at[zk(-k)], r_ed.at[k])
    for p in range(5):
        for s in range(nz):
            for j in range(4):
                r0 = (s * 4 + j) * 8
                f[p, r0:r0 + 8, :] = rz[s, j, p].astype(F32)
    for s in range(nz):
        for side in range(2):
            ge[s, side] = re[s, side].astype(F32)
    for side in range(2):
        for p in range(5):
            for s in range(nz):
                g2[side * 5 + p, 4 * s:4 * s + 4, :] = ge[s, side, pl.ds(p, 4, stride=5), :]
    for p in range(5):
        for r in range(8):
            xz[p, r + 1] = f[p, pl.ds(r, blk, stride=8), :].astype(BF16)
        xz[p, 0] = g2[p].astype(BF16)
        xz[p, 9] = g2[5 + p].astype(BF16)

    def x_part(yy):
        return X.at[c, pl.ds(1, 5), :, pl.ds(pl.multiple_of(yy * blk, blk), blk), :]

    for k in range(1, NYT):
        d = yk(k)
        sent.append(
            send(xz.at[:, pl.ds(2 * d, 4)], x_part(y), s_xy.at[k], r_xy.at[k], at(z, d, c, x))
        )
    own_y = local(xz.at[:, pl.ds(2 * y, 4)], x_part(y), loc.at[3])

    for k in range(1, NYT):
        d = wt.at[pl.ds(8 * x, 8), pl.ds(pl.multiple_of(yk(-k) * blk, blk), blk), :]
        recv(d, r_wy.at[k])

    def first(g):
        return wt.at[pl.ds(8 * g, 4)]

    def second(g):
        return wt.at[pl.ds(8 * g + 4, 3)]

    right, left = at(z, y, c, xr), at(z, y, c, xl)
    sent.append(send(first(x), first(x), s_wx.at[0], r_wx.at[0], right))
    sent.append(send(second(x), second(x), s_wx.at[1], r_wx.at[1], left))
    sent.append(send(second(x), second(x), s_wx.at[2], r_wx.at[2], right))
    sent.append(send(first(x), first(x), s_wx.at[3], r_wx.at[3], left))

    own_y.wait()
    for k in range(1, NYT):
        recv(x_part(yk(-k)), r_xy.at[k])

    @pl.when(x < NXT - 1)
    def _():
        send(X.at[c, 5], X.at[c, 0], s_xh.at[0], r_xh.at[0], right)

    @pl.when(x > 0)
    def _():
        send(X.at[c, 1], X.at[c, 6], s_xh.at[1], r_xh.at[1], left)

    own_planes = X.at[c, pl.ds(1, 5)]
    sent.append(send(own_planes, own_planes, s_cc.at[0], r_cc.at[0], sib))

    recv(first(xl), r_wx.at[0])
    sent.append(send(first(xl), first(xl), s_wx.at[4], r_wx.at[4], right))
    recv(second(xr), r_wx.at[1])
    sent.append(send(second(xr), second(xr), s_wx.at[5], r_wx.at[5], left))

    @pl.when(x > 0)
    def _():
        recv(X.at[c, 0], r_xh.at[0])
        send(X.at[c, 0], X.at[c, 0], s_xf.at[0], r_xf.at[0], sib)

    @pl.when(x < NXT - 1)
    def _():
        recv(X.at[c, 6], r_xh.at[1])
        send(X.at[c, 6], X.at[c, 6], s_xf.at[1], r_xf.at[1], sib)

    recv(X.at[1 - c, pl.ds(1, 5)], r_cc.at[0])

    @pl.when(x > 0)
    def _():
        recv(X.at[1 - c, 0], r_xf.at[0])

    @pl.when(x < NXT - 1)
    def _():
        recv(X.at[1 - c, 6], r_xf.at[1])

    xo = lax.rem(x + 2, NXT)
    recv(second(xl), r_wx.at[2])
    recv(first(xr), r_wx.at[3])
    recv(first(xo), r_wx.at[4])
    recv(second(xo), r_wx.at[5])

    bias = wt[8 * x + 7].astype(F32)[:, 0:1]
    lane = lax.broadcasted_iota(jnp.int32, (half, 128), 1)

    def compute(p):
        acc = None
        for a in range(3):
            for bq in range(3):
                t = 9 * a + 3 * bq
                lhs = jnp.concatenate([wt[tap_slot(t + q)] for q in range(3)], axis=0)
                rhs = jnp.concatenate(
                    [
                        jnp.concatenate([X[0, p + a, r + bq], X[1, p + a, r + bq]], axis=0)
                        for r in range(2)
                    ],
                    axis=1,
                )
                part = jnp.dot(lhs, rhs, preferred_element_type=F32)
                acc = part if acc is None else acc + part
        for r in range(2):
            cols = acc[:, 128 * r:128 * r + 128]
            low = jnp.where(lane == 0, 0.0, pltpu.roll(cols[0:half], 1, 1))
            high = jnp.where(lane == 127, 0.0, pltpu.roll(cols[2 * half:], 127, 1))
            total = low + cols[half:2 * half] + high + bias
            O[p, r] = jnp.where(total > 0, total, 0.3 * total).astype(BF16)

    def out_y(p):
        for k in range(1, NYT):
            d = yk(k)
            sent.append(
                send(
                    O.at[p, :, pl.ds(pl.multiple_of(d * blk, blk), blk), :],
                    oy.at[p, pl.ds(2 * y, 2)],
                    s_oy.at[p, k], r_oy.at[p, k], at(z, d, c, x),
                )
            )
        oy[p, pl.ds(2 * y, 2)] = O[p, :, pl.ds(yoff, blk), :]

    def out_z(p):
        for k in range(1, NYT):
            recv(oy.at[p, pl.ds(2 * yk(-k), 2)], r_oy.at[p, k])
        for r in range(8):
            fo[p, blk * r:blk * r + blk, :] = oy[p, r].astype(F32)
        for m in range(blk):
            oz[p, m // 4, m % 4] = fo[p, pl.ds(m, 8, stride=blk), :].astype(BF16)
        for k in range(1, nz):
            d = zk(k)
            sent.append(
                send(oz.at[p, d], out.at[:, p, z], s_oz.at[p, k], r_oz.at[p, k], at(d, y, c, x))
            )
        return local(oz.at[p, z], out.at[:, p, z], loc.at[4 + p])

    finals = []
    for p in range(5):
        compute(p)
        out_y(p)
        if p:
            finals.append(out_z(p - 1))
    finals.append(out_z(4))

    for cp in finals:
        cp.wait()
    for p in range(5):
        for k in range(1, nz):
            recv(out.at[:, p, zk(-k)], r_oz.at[p, k])
    for cp in sent:
        cp.wait_send()

    @pl.when(x < NXT - 1)
    def _():
        recv(X.at[c, 5], s_xh.at[0])
        recv(X.at[c, 6], s_xf.at[1])

    @pl.when(x > 0)
    def _():
        recv(X.at[c, 1], s_xh.at[1])
        recv(X.at[c, 0], s_xf.at[0])


def shards(nz, volume, weight, channel_bias):
    blk = 4 * nz
    half = NYT * blk
    n_in = 2 * half
    v = volume.reshape(4, 5, nz, 8, 128)
    w = weight.transpose(1, 0, 2)
    b = channel_bias.reshape(1, 4)
    vm = pltpu.VMEM
    dma = pltpu.SemaphoreType.DMA
    out = pl.pallas_call(
        functools.partial(kernel, nz),
        out_shape=jax.ShapeDtypeStruct((4, 5, nz, 8, 128), BF16),
        in_specs=[pl.BlockSpec(memory_space=pltpu.VMEM)] * 3,
        out_specs=pl.BlockSpec(memory_space=pltpu.VMEM),
        scratch_shapes=[
            vm((20 * 8 * nz, 128), F32),
            vm((nz, 2, 20, 128), BF16),
            vm((nz, 4, 5, 8, 128), BF16),
            vm((nz, 2, 20, 128), BF16),
            vm((5, blk * 8, 128), F32),
            vm((nz, 2, 20, 128), F32),
            vm((10, blk, 128), F32),
            vm((5, 10, blk, 128), BF16),
            vm((2, 7, 4, half, 128), BF16),
            vm((8, 4, n_in), BF16),
            vm((nz, 8, 4, n_in), BF16),
            vm((8, blk, n_in), F32),
            vm((32, half, n_in), BF16),
            vm((5, 2, half, 128), BF16),
            vm((5, 8, blk, 128), BF16),
            vm((5, 8 * blk, 128), F32),
            vm((5, nz, 4, 8, 128), BF16),
            dma((nz,)), dma((nz,)), dma((nz,)), dma((nz,)), dma((nz,)), dma((nz,)),
            dma((4,)), dma((4,)), dma((6,)), dma((6,)),
            dma((4,)), dma((4,)), dma((1,)), dma((1,)), dma((2,)), dma((2,)), dma((2,)), dma((2,)),
            dma((5, 4)), dma((5, 4)), dma((5, nz)), dma((5, nz)), dma((9,)),
        ],
        compiler_params=pltpu.CompilerParams(
            collective_id=0, has_side_effects=True, vmem_limit_bytes=40 * 1024 * 1024
        ),
        cost_estimate=pl.CostEstimate(
            flops=2 * 640 * n_in * n_in * 27, bytes_accessed=2 * v.size * 2, transcendentals=0
        ),
    )(v, w, b)
    return out.reshape(volume.shape)


def solution(mesh):
    nz = mesh.shape["ch"] // (2 * NYT)
    return jax.shard_map(
        functools.partial(shards, nz),
        mesh=mesh,
        in_specs=(P("ch", "sp", None, None), P("ch", None, None), P("ch")),
        out_specs=P("ch", "sp", None, None),
        check_vma=False,
    )
```

```python
import functools

import jax
import jax.numpy as jnp
from jax import lax
from jax.experimental import pallas as pl
from jax.experimental.pallas import tpu as pltpu
from jax.sharding import PartitionSpec as P

NYT = 4
NXT = 4
PLANES = (4, 0, 1, 2, 3)
OUT_LAG = 2
MESH = pl.DeviceIdType.MESH
F32 = jnp.float32
BF16 = jnp.bfloat16


def tap_slot(t):
    return t // 7 * 8 + t % 7 if t <= 20 else 24 + t - 20


def kernel(
    nz, v_hbm, w_hbm, b_hbm, out,
    v, b, fe, ed, rz, re, f, ge, g2, xz, X, ws, wz, wf, wt, O, oy, fo, oz,
    s_vz, r_vz, s_ed, r_ed, s_wz, r_wz, s_wy, r_wy, s_wx, r_wx,
    s_xy, r_xy, s_cc, r_cc, s_xh, r_xh, s_xf, r_xf, s_oy, r_oy, s_oz, r_oz, loc, loc_p,
):
    blk = 4 * nz
    half = NYT * blk
    ch = lax.axis_index("ch")
    x = lax.axis_index("sp")
    c = lax.rem(ch, 2)
    y = lax.rem(lax.div(ch, 2), NYT)
    z = lax.div(ch, 2 * NYT)

    def at(zz, yy, cc, xx):
        return {"ch": (zz * NYT + yy) * 2 + cc, "sp": xx}

    def zk(k):
        return lax.rem(z + k + nz, nz)

    def yk(k):
        return lax.rem(y + k + NYT, NYT)

    xl, xr = lax.rem(x + NXT - 1, NXT), lax.rem(x + 1, NXT)
    sib = at(z, y, 1 - c, x)
    right, left = at(z, y, c, xr), at(z, y, c, xl)

    def send(src, dst, ss, rs, to):
        cp = pltpu.make_async_remote_copy(
            src_ref=src, dst_ref=dst, send_sem=ss, recv_sem=rs, device_id=to, device_id_type=MESH
        )
        cp.start()
        return cp

    def recv(dst, sem):
        pltpu.make_async_copy(dst, dst, sem).wait()

    def local(src, dst, sem):
        cp = pltpu.make_async_copy(src, dst, sem)
        cp.start()
        return cp

    sent = []
    z_order = sorted(range(1, nz), key=lambda k: -min(k, nz - k))

    bar = pltpu.get_barrier_semaphore()
    peers = [at(zk(k), y, c, x) for k in range(1, nz)]
    peers += [at(z, yk(k), c, x) for k in range(1, NYT)]
    peers += [sib, left, right]
    start = jnp.minimum(7 * x, 20)
    loads = [
        local(v_hbm, v, loc.at[0]),
        local(b_hbm, b, loc.at[1]),
        local(w_hbm.at[pl.ds(start, 7)], ws.at[pl.ds(0, 7)], loc.at[2]),
    ]
    for p in peers:
        pl.semaphore_signal(bar, inc=1, device_id=p, device_id_type=MESH)

    @pl.when(x == 0)
    def _():
        X[:, 0] = jnp.zeros_like(X[:, 0])

    @pl.when(x == NXT - 1)
    def _():
        X[:, 6] = jnp.zeros_like(X[:, 6])

    n_in = 2 * half
    i = lax.broadcasted_iota(jnp.int32, (n_in, n_in), 0)
    o = lax.broadcasted_iota(jnp.int32, (n_in, n_in), 1)
    to = ((i >> 2) & 1) * half + ((i >> 3) & 3) * blk + (i >> 5) * 4 + (i & 3)
    perm = jnp.where(to == o, 1.0, 0.0).astype(BF16)

    loads[1].wait()
    bb = jnp.broadcast_to(b[...].astype(F32), (4, 4))
    eye = lax.broadcasted_iota(jnp.int32, (4, 4), 0) == lax.broadcasted_iota(jnp.int32, (4, 4), 1)
    col = jnp.sum(jnp.where(eye, bb, 0.0), axis=1, keepdims=True)
    ws[7] = jnp.broadcast_to(col, ws.shape[1:]).astype(BF16)

    loads[0].wait()
    for j in range(4):
        for p in range(5):
            base = (j * 5 + p) * nz * 8
            for k in range(nz):
                fe[base + 8 * k:base + 8 * k + 8, :] = v[j, p, k].astype(F32)
    zero_edge = jnp.zeros((20, 128), BF16)
    ed[0, 0] = zero_edge
    ed[nz - 1, 1] = zero_edge
    for k in range(1, nz):
        ed[k, 0] = fe[pl.ds(8 * k - 1, 20, stride=8 * nz), :].astype(BF16)
        ed[k - 1, 1] = fe[pl.ds(8 * k, 20, stride=8 * nz), :].astype(BF16)
    loads[2].wait()

    pl.semaphore_wait(bar, len(peers))

    for k in z_order:
        sent.append(send(ws, wz.at[z], s_wz.at[k], r_wz.at[k], at(zk(k), y, c, x)))
    own_w = local(ws, wz.at[z], loc.at[3])
    for k in z_order:
        d = zk(k)
        sent.append(send(ed.at[d], re.at[z], s_ed.at[k], r_ed.at[k], at(d, y, c, x)))
    own_e = local(ed.at[z], re.at[z], loc.at[4])
    own_v = {}
    for p in PLANES:
        for k in z_order:
            d = zk(k)
            sent.append(
                send(v.at[:, p, d], rz.at[p, z], s_vz.at[p, k], r_vz.at[p, k], at(d, y, c, x))
            )
        own_v[p] = local(v.at[:, p, z], rz.at[p, z], loc_p.at[p])

    own_w.wait()
    for k in z_order[::-1]:
        recv(wz.at[zk(-k)], r_wz.at[k])
    for t in range(8):
        for s in range(nz):
            wf[t, 4 * s:4 * s + 4, :] = wz[s, t].astype(F32)
    yoff = pl.multiple_of(y * blk, blk)
    for t in range(8):
        wt[8 * x + t, pl.ds(yoff, blk), :] = jnp.dot(
            wf[t].astype(BF16), perm, preferred_element_type=F32
        ).astype(BF16)

    def w_part(h, yy):
        return wt.at[pl.ds(8 * x + 4 * h, 4), pl.ds(pl.multiple_of(yy * blk, blk), blk), :]

    for h in range(2):
        for k in (2, 1, 3):
            mine = w_part(h, y)
            sent.append(send(mine, mine, s_wy.at[h, k], r_wy.at[h, k], at(z, yk(k), c, x)))

    def x_part(p, yy):
        return X.at[c, p + 1, :, pl.ds(pl.multiple_of(yy * blk, blk), blk), :]

    own_y = {}

    def volume_y(p):
        own_v[p].wait()
        for k in z_order[::-1]:
            recv(rz.at[p, zk(-k)], r_vz.at[p, k])
        for s in range(nz):
            for j in range(4):
                r0 = (s * 4 + j) * 8
                f[p, r0:r0 + 8, :] = rz[p, s, j].astype(F32)
        for r in range(8):
            xz[p, r + 1] = f[p, pl.ds(r, blk, stride=8), :].astype(BF16)
        for k in (2, 1, 3):
            d = yk(k)
            sent.append(
                send(
                    xz.at[p, pl.ds(2 * d, 4)], x_part(p, y), s_xy.at[p, k], r_xy.at[p, k],
                    at(z, d, c, x),
                )
            )
        own_y[p] = local(xz.at[p, pl.ds(2 * y, 4)], x_part(p, y), loc_p.at[5 + p])

    own_e.wait()
    for k in z_order[::-1]:
        recv(re.at[zk(-k)], r_ed.at[k])
    for s in range(nz):
        for side in range(2):
            ge[s, side] = re[s, side].astype(F32)
    for side in range(2):
        for p in range(5):
            for s in range(nz):
                g2[side * 5 + p, 4 * s:4 * s + 4, :] = ge[s, side, pl.ds(p, 4, stride=5), :]
            xz[p, 9 * side] = g2[side * 5 + p].astype(BF16)

    for p in PLANES[:3]:
        volume_y(p)

    def first(g):
        return wt.at[pl.ds(8 * g, 4)]

    def second(g):
        return wt.at[pl.ds(8 * g + 4, 3)]

    for k in range(1, NYT):
        recv(w_part(0, yk(-k)), r_wy.at[0, k])
    sent.append(send(first(x), first(x), s_wx.at[0], r_wx.at[0], right))
    for k in range(1, NYT):
        recv(w_part(1, yk(-k)), r_wy.at[1, k])
    sent.append(send(second(x), second(x), s_wx.at[1], r_wx.at[1], left))
    sent.append(send(second(x), second(x), s_wx.at[2], r_wx.at[2], right))
    sent.append(send(first(x), first(x), s_wx.at[3], r_wx.at[3], left))

    for p in PLANES[3:]:
        volume_y(p)

    for p in PLANES:
        own_y[p].wait()
        for k in range(1, NYT):
            recv(x_part(p, yk(-k)), r_xy.at[p, k])
        if p == 4:
            @pl.when(x < NXT - 1)
            def _():
                send(X.at[c, 5], X.at[c, 0], s_xh.at[0], r_xh.at[0], right)
        if p == 0:
            @pl.when(x > 0)
            def _():
                send(X.at[c, 1], X.at[c, 6], s_xh.at[1], r_xh.at[1], left)
        sent.append(send(X.at[c, p + 1], X.at[c, p + 1], s_cc.at[p], r_cc.at[p], sib))

    recv(first(xl), r_wx.at[0])
    sent.append(send(first(xl), first(xl), s_wx.at[4], r_wx.at[4], right))
    recv(second(xr), r_wx.at[1])
    sent.append(send(second(xr), second(xr), s_wx.at[5], r_wx.at[5], left))

    @pl.when(x > 0)
    def _():
        recv(X.at[c, 0], r_xh.at[0])
        send(X.at[c, 0], X.at[c, 0], s_xf.at[0], r_xf.at[0], sib)

    @pl.when(x < NXT - 1)
    def _():
        recv(X.at[c, 6], r_xh.at[1])
        send(X.at[c, 6], X.at[c, 6], s_xf.at[1], r_xf.at[1], sib)

    for p in PLANES:
        recv(X.at[1 - c, p + 1], r_cc.at[p])

    @pl.when(x > 0)
    def _():
        recv(X.at[1 - c, 0], r_xf.at[0])

    @pl.when(x < NXT - 1)
    def _():
        recv(X.at[1 - c, 6], r_xf.at[1])

    xo = lax.rem(x + 2, NXT)
    recv(second(xl), r_wx.at[2])
    recv(first(xr), r_wx.at[3])
    recv(first(xo), r_wx.at[4])
    recv(second(xo), r_wx.at[5])

    bias = wt[8 * x + 7].astype(F32)[:, 0:1]
    lane = lax.broadcasted_iota(jnp.int32, (half, 128), 1)

    def compute(p):
        acc = None
        for a in range(3):
            for bq in range(3):
                t = 9 * a + 3 * bq
                lhs = jnp.concatenate([wt[tap_slot(t + q)] for q in range(3)], axis=0)
                rhs = jnp.concatenate(
                    [
                        jnp.concatenate([X[0, p + a, r + bq], X[1, p + a, r + bq]], axis=0)
                        for r in range(2)
                    ],
                    axis=1,
                )
                part = jnp.dot(lhs, rhs, preferred_element_type=F32)
                acc = part if acc is None else acc + part
        for r in range(2):
            cols = acc[:, 128 * r:128 * r + 128]
            low = jnp.where(lane == 0, 0.0, pltpu.roll(cols[0:half], 1, 1))
            high = jnp.where(lane == 127, 0.0, pltpu.roll(cols[2 * half:], 127, 1))
            total = low + cols[half:2 * half] + high + bias
            O[p, r] = jnp.where(total > 0, total, 0.3 * total).astype(BF16)

    def out_y(p):
        for k in (2, 1, 3):
            d = yk(k)
            sent.append(
                send(
                    O.at[p, :, pl.ds(pl.multiple_of(d * blk, blk), blk), :],
                    oy.at[p, pl.ds(2 * y, 2)],
                    s_oy.at[p, k], r_oy.at[p, k], at(z, d, c, x),
                )
            )
        oy[p, pl.ds(2 * y, 2)] = O[p, :, pl.ds(yoff, blk), :]

    def out_z(p):
        for k in range(1, NYT):
            recv(oy.at[p, pl.ds(2 * yk(-k), 2)], r_oy.at[p, k])
        for r in range(8):
            fo[p, blk * r:blk * r + blk, :] = oy[p, r].astype(F32)
        for m in range(blk):
            oz[p, m // 4, m % 4] = fo[p, pl.ds(m, 8, stride=blk), :].astype(BF16)
        for k in z_order:
            d = zk(k)
            sent.append(
                send(oz.at[p, d], out.at[:, p, z], s_oz.at[p, k], r_oz.at[p, k], at(d, y, c, x))
            )
        return local(oz.at[p, z], out.at[:, p, z], loc_p.at[10 + p])

    finals = []
    order = [1, 2, 3, 0, 4]
    for n, p in enumerate(order):
        compute(p)
        out_y(p)
        if n >= OUT_LAG:
            finals.append(out_z(order[n - OUT_LAG]))
    for p in order[5 - OUT_LAG:]:
        finals.append(out_z(p))

    for cp in finals:
        cp.wait()
    for p in order:
        for k in range(1, nz):
            recv(out.at[:, p, zk(-k)], r_oz.at[p, k])
    for cp in sent:
        cp.wait_send()

    @pl.when(x < NXT - 1)
    def _():
        recv(X.at[c, 5], s_xh.at[0])
        recv(X.at[c, 6], s_xf.at[1])

    @pl.when(x > 0)
    def _():
        recv(X.at[c, 1], s_xh.at[1])
        recv(X.at[c, 0], s_xf.at[0])


def shards(nz, volume, weight, channel_bias):
    blk = 4 * nz
    half = NYT * blk
    n_in = 2 * half
    v = volume.reshape(4, 5, nz, 8, 128)
    w = weight.transpose(1, 0, 2)
    b = channel_bias.reshape(1, 4)
    vm = pltpu.VMEM
    dma = pltpu.SemaphoreType.DMA
    out = pl.pallas_call(
        functools.partial(kernel, nz),
        out_shape=jax.ShapeDtypeStruct((4, 5, nz, 8, 128), BF16),
        in_specs=[pl.BlockSpec(memory_space=pl.ANY)] * 3,
        out_specs=pl.BlockSpec(memory_space=pltpu.VMEM),
        scratch_shapes=[
            vm((4, 5, nz, 8, 128), BF16),
            vm((1, 4), BF16),
            vm((20 * 8 * nz, 128), F32),
            vm((nz, 2, 20, 128), BF16),
            vm((5, nz, 4, 8, 128), BF16),
            vm((nz, 2, 20, 128), BF16),
            vm((5, blk * 8, 128), F32),
            vm((nz, 2, 20, 128), F32),
            vm((10, blk, 128), F32),
            vm((5, 10, blk, 128), BF16),
            vm((2, 7, 4, half, 128), BF16),
            vm((8, 4, n_in), BF16),
            vm((nz, 8, 4, n_in), BF16),
            vm((8, blk, n_in), F32),
            vm((32, half, n_in), BF16),
            vm((5, 2, half, 128), BF16),
            vm((5, 8, blk, 128), BF16),
            vm((5, 8 * blk, 128), F32),
            vm((5, nz, 4, 8, 128), BF16),
            dma((5, nz)), dma((5, nz)), dma((nz,)), dma((nz,)), dma((nz,)), dma((nz,)),
            dma((2, 4)), dma((2, 4)), dma((6,)), dma((6,)),
            dma((5, 4)), dma((5, 4)), dma((5,)), dma((5,)), dma((2,)), dma((2,)), dma((2,)), dma((2,)),
            dma((5, 4)), dma((5, 4)), dma((5, nz)), dma((5, nz)), dma((5,)), dma((15,)),
        ],
        compiler_params=pltpu.CompilerParams(
            collective_id=0, has_side_effects=True, vmem_limit_bytes=63 * 1024 * 1024
        ),
        cost_estimate=pl.CostEstimate(
            flops=2 * 640 * n_in * n_in * 27, bytes_accessed=2 * v.size * 2, transcendentals=0
        ),
    )(v, w, b)
    return out.reshape(volume.shape)


def solution(mesh):
    nz = mesh.shape["ch"] // (2 * NYT)
    return jax.shard_map(
        functools.partial(shards, nz),
        mesh=mesh,
        in_specs=(P("ch", "sp", None, None), P("ch", None, None), P("ch")),
        out_specs=P("ch", "sp", None, None),
        check_vma=False,
    )
```

```python
import functools

import jax
import jax.numpy as jnp
from jax import lax
from jax.experimental import pallas as pl
from jax.experimental.pallas import tpu as pltpu
from jax.sharding import PartitionSpec as P

NYT = 4
NXT = 4
PLANES = (4, 0, 1, 2, 3)
OUT_LAG = 3
N1 = 5
STEPS = "v4 v0 f1 f3 g0 v1 f2 v2 v3 g1 g3 c4 c0 g2 c1 c2 c3 h".split()
MESH = pl.DeviceIdType.MESH
F32 = jnp.float32
BF16 = jnp.bfloat16


def tap_slot(t):
    return (t // 7, t % 7) if t <= 20 else (3, t - 20)


def kernel(
    nz, v_hbm, w_hbm, b_hbm, out,
    v, b, fe, ed, rz, re, f, ge, g2, xz, X, ws, wz, wf, wt, O, oy, fo, oz,
    s_vz, r_vz, s_ed, r_ed, s_wz, r_wz, s_wa, r_wa, s_wb, r_wb,
    s_xy, r_xy, s_cc, r_cc, s_xh, r_xh, s_xf, r_xf, s_oy, r_oy, s_oz, r_oz, loc, loc_p,
):
    blk = 4 * nz
    half = NYT * blk
    ch = lax.axis_index("ch")
    x = lax.axis_index("sp")
    c = lax.rem(ch, 2)
    y = lax.rem(lax.div(ch, 2), NYT)
    z = lax.div(ch, 2 * NYT)

    def at(zz, yy, cc, xx):
        return {"ch": (zz * NYT + yy) * 2 + cc, "sp": xx}

    def zk(k):
        return lax.rem(z + k + nz, nz)

    def yk(k):
        return lax.rem(y + k + NYT, NYT)

    xl, xr = lax.rem(x + NXT - 1, NXT), lax.rem(x + 1, NXT)
    sib = at(z, y, 1 - c, x)
    right, left = at(z, y, c, xr), at(z, y, c, xl)

    def send(src, dst, ss, rs, to):
        cp = pltpu.make_async_remote_copy(
            src_ref=src, dst_ref=dst, send_sem=ss, recv_sem=rs, device_id=to, device_id_type=MESH
        )
        cp.start()
        return cp

    def recv(dst, sem):
        pltpu.make_async_copy(dst, dst, sem).wait()

    def local(src, dst, sem):
        cp = pltpu.make_async_copy(src, dst, sem)
        cp.start()
        return cp

    sent = []
    z_order = sorted(range(1, nz), key=lambda k: -min(k, nz - k))

    bar = pltpu.get_barrier_semaphore()
    peers = [at(zk(k), y, c, x) for k in range(1, nz)]
    peers += [at(z, yk(k), c, x) for k in range(1, NYT)]
    peers += [at(z, y, c, lax.rem(x + k, NXT)) for k in range(1, NXT)]
    peers += [sib]
    start = jnp.minimum(7 * x, 20)
    loads = [
        local(v_hbm, v, loc.at[0]),
        local(b_hbm, b, loc.at[1]),
        local(w_hbm.at[pl.ds(start, 7)], ws.at[pl.ds(0, 7)], loc.at[2]),
    ]
    for p in peers:
        pl.semaphore_signal(bar, inc=1, device_id=p, device_id_type=MESH)

    @pl.when(x == 0)
    def _():
        X[:, 0] = jnp.zeros_like(X[:, 0])

    @pl.when(x == NXT - 1)
    def _():
        X[:, 6] = jnp.zeros_like(X[:, 6])

    n_in = 2 * half
    i = lax.broadcasted_iota(jnp.int32, (n_in, n_in), 0)
    o = lax.broadcasted_iota(jnp.int32, (n_in, n_in), 1)
    to = ((i >> 2) & 1) * half + ((i >> 3) & 3) * blk + (i >> 5) * 4 + (i & 3)
    perm = jnp.where(to == o, 1.0, 0.0).astype(BF16)

    loads[1].wait()
    bb = jnp.broadcast_to(b[...].astype(F32), (4, 4))
    eye = lax.broadcasted_iota(jnp.int32, (4, 4), 0) == lax.broadcasted_iota(jnp.int32, (4, 4), 1)
    col = jnp.sum(jnp.where(eye, bb, 0.0), axis=1, keepdims=True)
    ws[7] = jnp.broadcast_to(col, ws.shape[1:]).astype(BF16)

    loads[0].wait()
    for j in range(4):
        for p in range(5):
            base = (j * 5 + p) * nz * 8
            for k in range(nz):
                fe[base + 8 * k:base + 8 * k + 8, :] = v[j, p, k].astype(F32)
    zero_edge = jnp.zeros((20, 128), BF16)
    ed[0, 0] = zero_edge
    ed[nz - 1, 1] = zero_edge
    for k in range(1, nz):
        ed[k, 0] = fe[pl.ds(8 * k - 1, 20, stride=8 * nz), :].astype(BF16)
        ed[k - 1, 1] = fe[pl.ds(8 * k, 20, stride=8 * nz), :].astype(BF16)
    loads[2].wait()

    pl.semaphore_wait(bar, len(peers))

    for k in z_order:
        sent.append(send(ws, wz.at[z], s_wz.at[k], r_wz.at[k], at(zk(k), y, c, x)))
    own_w = local(ws, wz.at[z], loc.at[3])
    for k in z_order:
        d = zk(k)
        sent.append(send(ed.at[d], re.at[z], s_ed.at[k], r_ed.at[k], at(d, y, c, x)))
    own_e = local(ed.at[z], re.at[z], loc.at[4])
    own_v = {}
    for p in PLANES:
        for k in z_order:
            d = zk(k)
            sent.append(
                send(v.at[:, p, d], rz.at[p, z], s_vz.at[p, k], r_vz.at[p, k], at(d, y, c, x))
            )
        own_v[p] = local(v.at[:, p, z], rz.at[p, z], loc_p.at[p])

    own_w.wait()
    for k in z_order[::-1]:
        recv(wz.at[zk(-k)], r_wz.at[k])
    for t in range(8):
        for s in range(nz):
            wf[t, 4 * s:4 * s + 4, :] = wz[s, t].astype(F32)
    yoff = pl.multiple_of(y * blk, blk)
    for t in range(8):
        wt[x, t, pl.ds(yoff, blk), :] = jnp.dot(
            wf[t].astype(BF16), perm, preferred_element_type=F32
        ).astype(BF16)

    def rows(yy):
        return pl.ds(pl.multiple_of(yy * blk, blk), blk)

    def part_rows(yy, h):
        if h is None:
            return rows(yy)
        return pl.ds(pl.multiple_of(yy * blk + h * (blk // 2), blk // 2), blk // 2)

    def w1(g, yy, h=None):
        return wt.at[g, pl.ds(0, N1), part_rows(yy, h), :]

    def w2(g, yy, h=None):
        return wt.at[g, pl.ds(N1, 7 - N1), part_rows(yy, h), :]

    def w3(yy):
        return wt.at[x, 7, rows(yy), :]

    def xk(k):
        return lax.rem(x + k + NXT, NXT)

    for k in (2, 1, 3):
        sent.append(send(w1(x, y), w1(x, y), s_wa.at[0, k], r_wa.at[0, k], at(z, yk(k), c, x)))
        sent.append(send(w2(x, y), w2(x, y), s_wa.at[1, k], r_wa.at[1, k], at(z, y, c, xk(k))))
        sent.append(send(w3(y), w3(y), s_wa.at[2, k], r_wa.at[2, k], at(z, yk(k), c, x)))

    def forward(q):
        yq, xq = yk(-q), xk(-q)
        if q:
            recv(w1(x, yq), r_wa.at[0, q])
        for k in (1, 3):
            to = at(z, y, c, xk(k))
            sent.append(send(w1(x, yq), w1(x, yq), s_wb.at[0, q, k], r_wb.at[0, q, k], to))
        if q:
            recv(w2(xq, y), r_wa.at[1, q])
        for k in (1, 3):
            to = at(z, yk(k), c, x)
            sent.append(send(w2(xq, y), w2(xq, y), s_wb.at[1, q, k], r_wb.at[1, q, k], to))

    def pass_on(q):
        yq, xq = yk(-q), xk(-q)
        recv(w1(xk(-1), yq), r_wb.at[0, q, 1])
        half0 = w1(xk(-1), yq, 0)
        sent.append(send(half0, half0, s_wb.at[0, q, 2], r_wb.at[0, q, 2], at(z, y, c, xk(1))))
        recv(w1(xk(1), yq), r_wb.at[0, q, 3])
        half1 = w1(xk(1), yq, 1)
        sent.append(send(half1, half1, s_wb.at[0, q, 0], r_wb.at[0, q, 0], at(z, y, c, xk(-1))))
        recv(w2(xq, yk(-1)), r_wb.at[1, q, 1])
        half2 = w2(xq, yk(-1), 0)
        sent.append(send(half2, half2, s_wb.at[1, q, 2], r_wb.at[1, q, 2], at(z, yk(1), c, x)))
        recv(w2(xq, yk(1)), r_wb.at[1, q, 3])
        half3 = w2(xq, yk(1), 1)
        sent.append(send(half3, half3, s_wb.at[1, q, 0], r_wb.at[1, q, 0], at(z, yk(-1), c, x)))

    forward(0)

    def x_part(p, yy):
        return X.at[c, p + 1, :, pl.ds(pl.multiple_of(yy * blk, blk), blk), :]

    own_y = {}

    def volume_y(p):
        own_v[p].wait()
        for k in z_order[::-1]:
            recv(rz.at[p, zk(-k)], r_vz.at[p, k])
        for s in range(nz):
            for j in range(4):
                r0 = (s * 4 + j) * 8
                f[p, r0:r0 + 8, :] = rz[p, s, j].astype(F32)
        for r in range(8):
            xz[p, r + 1] = f[p, pl.ds(r, blk, stride=8), :].astype(BF16)
        for k in (2, 1, 3):
            d = yk(k)
            sent.append(
                send(
                    xz.at[p, pl.ds(2 * d, 4)], x_part(p, y), s_xy.at[p, k], r_xy.at[p, k],
                    at(z, d, c, x),
                )
            )
        own_y[p] = local(xz.at[p, pl.ds(2 * y, 4)], x_part(p, y), loc_p.at[5 + p])

    own_e.wait()
    for k in z_order[::-1]:
        recv(re.at[zk(-k)], r_ed.at[k])
    for s in range(nz):
        for side in range(2):
            ge[s, side] = re[s, side].astype(F32)
    for side in range(2):
        for p in range(5):
            for s in range(nz):
                g2[side * 5 + p, 4 * s:4 * s + 4, :] = ge[s, side, pl.ds(p, 4, stride=5), :]
            xz[p, 9 * side] = g2[side * 5 + p].astype(BF16)

    def share(p):
        own_y[p].wait()
        for k in range(1, NYT):
            recv(x_part(p, yk(-k)), r_xy.at[p, k])
        if p == 4:
            @pl.when(x < NXT - 1)
            def _():
                send(X.at[c, 5], X.at[c, 0], s_xh.at[0], r_xh.at[0], right)
        if p == 0:
            @pl.when(x > 0)
            def _():
                send(X.at[c, 1], X.at[c, 6], s_xh.at[1], r_xh.at[1], left)
        sent.append(send(X.at[c, p + 1], X.at[c, p + 1], s_cc.at[p], r_cc.at[p], sib))

    def halo():
        @pl.when(x > 0)
        def _():
            recv(X.at[c, 0], r_xh.at[0])
            send(X.at[c, 0], X.at[c, 0], s_xf.at[0], r_xf.at[0], sib)

        @pl.when(x < NXT - 1)
        def _():
            recv(X.at[c, 6], r_xh.at[1])
            send(X.at[c, 6], X.at[c, 6], s_xf.at[1], r_xf.at[1], sib)

    for step in STEPS:
        if step[0] == "v":
            volume_y(int(step[1]))
        elif step[0] == "f":
            forward(int(step[1]))
        elif step[0] == "g":
            pass_on(int(step[1]))
        elif step[0] == "c":
            share(int(step[1]))
        else:
            halo()

    for p in PLANES:
        recv(X.at[1 - c, p + 1], r_cc.at[p])

    for q in range(NXT):
        for h, k in ((0, 2), (1, 0)):
            recv(w1(xk(2), yk(-q), h), r_wb.at[0, q, k])
            recv(w2(xk(-q), yk(2), h), r_wb.at[1, q, k])
    for k in range(1, NYT):
        recv(w3(yk(-k)), r_wa.at[2, k])

    def halo_wait():
        @pl.when(x > 0)
        def _():
            recv(X.at[1 - c, 0], r_xf.at[0])

        @pl.when(x < NXT - 1)
        def _():
            recv(X.at[1 - c, 6], r_xf.at[1])

    bias = wt[x, 7].astype(F32)[:, 0:1]
    lane = lax.broadcasted_iota(jnp.int32, (half, 128), 1)

    def compute(p):
        acc = None
        for a in range(3):
            for bq in range(3):
                t = 9 * a + 3 * bq
                lhs = jnp.concatenate([wt[tap_slot(t + q)] for q in range(3)], axis=0)
                rhs = jnp.concatenate(
                    [
                        jnp.concatenate([X[0, p + a, r + bq], X[1, p + a, r + bq]], axis=0)
                        for r in range(2)
                    ],
                    axis=1,
                )
                part = jnp.dot(lhs, rhs, preferred_element_type=F32)
                acc = part if acc is None else acc + part
        for r in range(2):
            cols = acc[:, 128 * r:128 * r + 128]
            low = jnp.where(lane == 0, 0.0, pltpu.roll(cols[0:half], 1, 1))
            high = jnp.where(lane == 127, 0.0, pltpu.roll(cols[2 * half:], 127, 1))
            total = low + cols[half:2 * half] + high + bias
            O[p, r] = jnp.where(total > 0, total, 0.3 * total).astype(BF16)

    def out_y(p):
        for k in (2, 1, 3):
            d = yk(k)
            sent.append(
                send(
                    O.at[p, :, pl.ds(pl.multiple_of(d * blk, blk), blk), :],
                    oy.at[p, pl.ds(2 * y, 2)],
                    s_oy.at[p, k], r_oy.at[p, k], at(z, d, c, x),
                )
            )
        oy[p, pl.ds(2 * y, 2)] = O[p, :, pl.ds(yoff, blk), :]

    def out_z(p):
        for k in range(1, NYT):
            recv(oy.at[p, pl.ds(2 * yk(-k), 2)], r_oy.at[p, k])
        for r in range(8):
            fo[p, blk * r:blk * r + blk, :] = oy[p, r].astype(F32)
        for m in range(blk):
            oz[p, m // 4, m % 4] = fo[p, pl.ds(m, 8, stride=blk), :].astype(BF16)
        for k in z_order:
            d = zk(k)
            sent.append(
                send(oz.at[p, d], out.at[:, p, z], s_oz.at[p, k], r_oz.at[p, k], at(d, y, c, x))
            )
        return local(oz.at[p, z], out.at[:, p, z], loc_p.at[10 + p])

    finals = []
    order = [1, 2, 3, 0, 4]
    for n, p in enumerate(order):
        if n == 3:
            halo_wait()
        compute(p)
        out_y(p)
        if n >= OUT_LAG:
            finals.append(out_z(order[n - OUT_LAG]))
    for p in order[5 - OUT_LAG:]:
        finals.append(out_z(p))

    for cp in finals:
        cp.wait()
    for p in order:
        for k in range(1, nz):
            recv(out.at[:, p, zk(-k)], r_oz.at[p, k])
    for cp in sent:
        cp.wait_send()

    @pl.when(x < NXT - 1)
    def _():
        recv(X.at[c, 5], s_xh.at[0])
        recv(X.at[c, 6], s_xf.at[1])

    @pl.when(x > 0)
    def _():
        recv(X.at[c, 1], s_xh.at[1])
        recv(X.at[c, 0], s_xf.at[0])


def shards(nz, volume, weight, channel_bias):
    blk = 4 * nz
    half = NYT * blk
    n_in = 2 * half
    v = volume.reshape(4, 5, nz, 8, 128)
    w = weight.transpose(1, 0, 2)
    b = channel_bias.reshape(1, 4)
    vm = pltpu.VMEM
    dma = pltpu.SemaphoreType.DMA
    out = pl.pallas_call(
        functools.partial(kernel, nz),
        out_shape=pltpu.VMEM((4, 5, nz, 8, 128), BF16),
        in_specs=[pl.BlockSpec(memory_space=pl.ANY)] * 3,
        out_specs=pl.BlockSpec(memory_space=pltpu.VMEM),
        scratch_shapes=[
            vm((4, 5, nz, 8, 128), BF16),
            vm((1, 4), BF16),
            vm((20 * 8 * nz, 128), F32),
            vm((nz, 2, 20, 128), BF16),
            vm((5, nz, 4, 8, 128), BF16),
            vm((nz, 2, 20, 128), BF16),
            vm((5, blk * 8, 128), F32),
            vm((nz, 2, 20, 128), F32),
            vm((10, blk, 128), F32),
            vm((5, 10, blk, 128), BF16),
            vm((2, 7, 4, half, 128), BF16),
            vm((8, 4, n_in), BF16),
            vm((nz, 8, 4, n_in), BF16),
            vm((8, blk, n_in), F32),
            vm((4, 8, half, n_in), BF16),
            vm((5, 2, half, 128), BF16),
            vm((5, 8, blk, 128), BF16),
            vm((5, 8 * blk, 128), F32),
            vm((5, nz, 4, 8, 128), BF16),
            dma((5, nz)), dma((5, nz)), dma((nz,)), dma((nz,)), dma((nz,)), dma((nz,)),
            dma((3, 4)), dma((3, 4)), dma((2, 4, 4)), dma((2, 4, 4)),
            dma((5, 4)), dma((5, 4)), dma((5,)), dma((5,)), dma((2,)), dma((2,)), dma((2,)), dma((2,)),
            dma((5, 4)), dma((5, 4)), dma((5, nz)), dma((5, nz)), dma((5,)), dma((15,)),
        ],
        compiler_params=pltpu.CompilerParams(
            collective_id=0, has_side_effects=True, vmem_limit_bytes=56 * 1024 * 1024
        ),
        cost_estimate=pl.CostEstimate(
            flops=2 * 640 * n_in * n_in * 27, bytes_accessed=2 * v.size * 2, transcendentals=0
        ),
    )(v, w, b)
    return out.reshape(volume.shape)


def solution(mesh):
    nz = mesh.shape["ch"] // (2 * NYT)
    return jax.shard_map(
        functools.partial(shards, nz),
        mesh=mesh,
        in_specs=(P("ch", "sp", None, None), P("ch", None, None), P("ch")),
        out_specs=P("ch", "sp", None, None),
        check_vma=False,
    )
```

```python
import functools

import jax
import jax.numpy as jnp
from jax import lax
from jax.experimental import pallas as pl
from jax.experimental.pallas import tpu as pltpu
from jax.sharding import PartitionSpec as P

NYT = 4
NXT = 4
PLANES = (4, 0, 1, 2, 3)
OUT_LAG = 3
N1 = 5
STEPS = ("v4", "v0", "f1", "f3", "g0", "v1", "f2", "v2", "v3", "g1", "g3", "c4", "c0", "g2", "c1", "c2", "c3", "h")
MESH = pl.DeviceIdType.MESH
F32 = jnp.float32
BF16 = jnp.bfloat16


def tap_slot(t):
    return (t // 7, t % 7) if t <= 20 else (3, t - 20)


def kernel(
    nz, v_hbm, w_hbm, b_hbm, out,
    b, va, fe, et, rz, f, g2, xz, X, ws, wz, wf, wt, O, oy, fo, oz,
    s_vz, r_vz, s_wz, r_wz, s_wa, r_wa, s_wb, r_wb,
    s_xy, r_xy, s_cc, r_cc, s_xh, r_xh, s_xf, r_xf, s_oy, r_oy, s_oz, r_oz, loc, loc_p,
):
    blk = 4 * nz
    half = NYT * blk
    ch = lax.axis_index("ch")
    x = lax.axis_index("sp")
    c = lax.rem(ch, 2)
    y = lax.rem(lax.div(ch, 2), NYT)
    z = lax.div(ch, 2 * NYT)

    def at(zz, yy, cc, xx):
        return {"ch": (zz * NYT + yy) * 2 + cc, "sp": xx}

    def zk(k):
        return lax.rem(z + k + nz, nz)

    def yk(k):
        return lax.rem(y + k + NYT, NYT)

    xl, xr = lax.rem(x + NXT - 1, NXT), lax.rem(x + 1, NXT)
    sib = at(z, y, 1 - c, x)
    right, left = at(z, y, c, xr), at(z, y, c, xl)

    def send(src, dst, ss, rs, to):
        cp = pltpu.make_async_remote_copy(
            src_ref=src, dst_ref=dst, send_sem=ss, recv_sem=rs, device_id=to, device_id_type=MESH
        )
        cp.start()
        return cp

    def recv(dst, sem):
        pltpu.make_async_copy(dst, dst, sem).wait()

    def local(src, dst, sem):
        cp = pltpu.make_async_copy(src, dst, sem)
        cp.start()
        return cp

    sent = []
    z_order = sorted(range(1, nz), key=lambda k: -min(k, nz - k))

    bar = pltpu.get_barrier_semaphore()
    peers = [at(zk(k), y, c, x) for k in range(1, nz)]
    peers += [at(z, yk(k), c, x) for k in range(1, NYT)]
    peers += [at(z, y, c, lax.rem(x + k, NXT)) for k in range(1, NXT)]
    peers += [sib]
    start = jnp.minimum(7 * x, 20)
    loads = [
        local(w_hbm.at[pl.ds(start, 7)], ws.at[pl.ds(0, 7)], loc.at[0]),
        local(b_hbm, b, loc.at[1]),
    ]
    v_loads = [local(v_hbm.at[j], va.at[:, :, j], loc_p.at[15 + j]) for j in range(4)]
    for p in peers:
        pl.semaphore_signal(bar, inc=1, device_id=p, device_id_type=MESH)

    @pl.when(x == 0)
    def _():
        X[:, 0] = jnp.zeros_like(X[:, 0])

    @pl.when(x == NXT - 1)
    def _():
        X[:, 6] = jnp.zeros_like(X[:, 6])

    n_in = 2 * half
    i = lax.broadcasted_iota(jnp.int32, (n_in, n_in), 0)
    o = lax.broadcasted_iota(jnp.int32, (n_in, n_in), 1)
    to = ((i >> 2) & 1) * half + ((i >> 3) & 3) * blk + (i >> 5) * 4 + (i & 3)
    perm = jnp.where(to == o, 1.0, 0.0).astype(BF16)

    loads[1].wait()
    bb = jnp.broadcast_to(b[...].astype(F32), (4, 4))
    eye = lax.broadcasted_iota(jnp.int32, (4, 4), 0) == lax.broadcasted_iota(jnp.int32, (4, 4), 1)
    col = jnp.sum(jnp.where(eye, bb, 0.0), axis=1, keepdims=True)
    ws[7] = jnp.broadcast_to(col, ws.shape[1:]).astype(BF16)

    loads[0].wait()

    pl.semaphore_wait(bar, len(peers))

    for k in z_order:
        sent.append(send(ws, wz.at[z], s_wz.at[k], r_wz.at[k], at(zk(k), y, c, x)))
    own_w = local(ws, wz.at[z], loc.at[3])
    for cp in v_loads:
        cp.wait()
    own_v = {}
    for p in PLANES:
        for d in range(nz):
            for j in range(4):
                r0 = (d * 4 + j) * 8
                fe[p, r0:r0 + 8, :] = va[p, d, j].astype(F32)
        for d in range(nz):
            et[p, d, 0:4, :] = (
                fe[p, pl.ds((d - 1) * 32 + 7, 4, stride=8), :] if d else jnp.zeros((4, 128), F32)
            )
            et[p, d, 4:8, :] = (
                fe[p, pl.ds((d + 1) * 32, 4, stride=8), :] if d < nz - 1 else jnp.zeros((4, 128), F32)
            )
            va[p, d, 4] = et[p, d].astype(BF16)
        for k in z_order:
            d = zk(k)
            sent.append(
                send(va.at[p, d], rz.at[p, z], s_vz.at[p, k], r_vz.at[p, k], at(d, y, c, x))
            )
        own_v[p] = local(va.at[p, z], rz.at[p, z], loc_p.at[p])

    own_w.wait()
    for k in z_order[::-1]:
        recv(wz.at[zk(-k)], r_wz.at[k])
    for t in range(8):
        for s in range(nz):
            wf[t, 4 * s:4 * s + 4, :] = wz[s, t].astype(F32)
    yoff = pl.multiple_of(y * blk, blk)
    for t in range(8):
        wt[x, t, pl.ds(yoff, blk), :] = jnp.dot(
            wf[t].astype(BF16), perm, preferred_element_type=F32
        ).astype(BF16)

    def rows(yy):
        return pl.ds(pl.multiple_of(yy * blk, blk), blk)

    def part_rows(yy, h):
        if h is None:
            return rows(yy)
        return pl.ds(pl.multiple_of(yy * blk + h * (blk // 2), blk // 2), blk // 2)

    def w1(g, yy, h=None):
        return wt.at[g, pl.ds(0, N1), part_rows(yy, h), :]

    def w2(g, yy, h=None):
        return wt.at[g, pl.ds(N1, 7 - N1), part_rows(yy, h), :]

    def w3(yy):
        return wt.at[x, 7, rows(yy), pl.ds(0, min(128, n_in))]

    def xk(k):
        return lax.rem(x + k + NXT, NXT)

    for k in (1, 3, 2):
        sent.append(send(w1(x, y), w1(x, y), s_wa.at[0, k], r_wa.at[0, k], at(z, yk(k), c, x)))
        sent.append(send(w2(x, y), w2(x, y), s_wa.at[1, k], r_wa.at[1, k], at(z, y, c, xk(k))))
        sent.append(send(w3(y), w3(y), s_wa.at[2, k], r_wa.at[2, k], at(z, yk(k), c, x)))

    def forward(q):
        yq, xq = yk(-q), xk(-q)
        if q:
            recv(w1(x, yq), r_wa.at[0, q])
        for k in (1, 3):
            to = at(z, y, c, xk(k))
            sent.append(send(w1(x, yq), w1(x, yq), s_wb.at[0, q, k], r_wb.at[0, q, k], to))
        if q:
            recv(w2(xq, y), r_wa.at[1, q])
        for k in (1, 3):
            to = at(z, yk(k), c, x)
            sent.append(send(w2(xq, y), w2(xq, y), s_wb.at[1, q, k], r_wb.at[1, q, k], to))

    def pass_on(q):
        yq, xq = yk(-q), xk(-q)
        recv(w1(xk(-1), yq), r_wb.at[0, q, 1])
        half0 = w1(xk(-1), yq, 0)
        sent.append(send(half0, half0, s_wb.at[0, q, 2], r_wb.at[0, q, 2], at(z, y, c, xk(1))))
        recv(w1(xk(1), yq), r_wb.at[0, q, 3])
        half1 = w1(xk(1), yq, 1)
        sent.append(send(half1, half1, s_wb.at[0, q, 0], r_wb.at[0, q, 0], at(z, y, c, xk(-1))))
        recv(w2(xq, yk(-1)), r_wb.at[1, q, 1])
        half2 = w2(xq, yk(-1), 0)
        sent.append(send(half2, half2, s_wb.at[1, q, 2], r_wb.at[1, q, 2], at(z, yk(1), c, x)))
        recv(w2(xq, yk(1)), r_wb.at[1, q, 3])
        half3 = w2(xq, yk(1), 1)
        sent.append(send(half3, half3, s_wb.at[1, q, 0], r_wb.at[1, q, 0], at(z, yk(-1), c, x)))

    forward(0)

    def x_part(p, yy):
        return X.at[c, p + 1, :, pl.ds(pl.multiple_of(yy * blk, blk), blk), :]

    own_y = {}

    def volume_y(p):
        own_v[p].wait()
        for k in z_order[::-1]:
            recv(rz.at[p, zk(-k)], r_vz.at[p, k])
        for s in range(nz):
            for j in range(4):
                r0 = (s * 4 + j) * 8
                f[p, r0:r0 + 8, :] = rz[p, s, j].astype(F32)
        for s in range(nz):
            e = rz[p, s, 4].astype(F32)
            g2[p, 4 * s:4 * s + 4, :] = e[0:4]
            g2[5 + p, 4 * s:4 * s + 4, :] = e[4:8]
        xz[p, 0] = g2[p].astype(BF16)
        xz[p, 9] = g2[5 + p].astype(BF16)
        for r in range(8):
            xz[p, r + 1] = f[p, pl.ds(r, blk, stride=8), :].astype(BF16)
        for k in (2, 1, 3):
            d = yk(k)
            sent.append(
                send(
                    xz.at[p, pl.ds(2 * d, 4)], x_part(p, y), s_xy.at[p, k], r_xy.at[p, k],
                    at(z, d, c, x),
                )
            )
        own_y[p] = local(xz.at[p, pl.ds(2 * y, 4)], x_part(p, y), loc_p.at[5 + p])

    def share(p):
        own_y[p].wait()
        for k in range(1, NYT):
            recv(x_part(p, yk(-k)), r_xy.at[p, k])
        if p == 4:
            @pl.when(x < NXT - 1)
            def _():
                send(X.at[c, 5], X.at[c, 0], s_xh.at[0], r_xh.at[0], right)
        if p == 0:
            @pl.when(x > 0)
            def _():
                send(X.at[c, 1], X.at[c, 6], s_xh.at[1], r_xh.at[1], left)
        sent.append(send(X.at[c, p + 1], X.at[c, p + 1], s_cc.at[p], r_cc.at[p], sib))

    def halo():
        @pl.when(x > 0)
        def _():
            recv(X.at[c, 0], r_xh.at[0])
            send(X.at[c, 0], X.at[c, 0], s_xf.at[0], r_xf.at[0], sib)

        @pl.when(x < NXT - 1)
        def _():
            recv(X.at[c, 6], r_xh.at[1])
            send(X.at[c, 6], X.at[c, 6], s_xf.at[1], r_xf.at[1], sib)

    for step in STEPS:
        if step[0] == "v":
            volume_y(int(step[1]))
        elif step[0] == "f":
            forward(int(step[1]))
        elif step[0] == "g":
            pass_on(int(step[1]))
        elif step[0] == "c":
            share(int(step[1]))
        else:
            halo()

    for p in PLANES:
        recv(X.at[1 - c, p + 1], r_cc.at[p])

    for q in range(NXT):
        for h, k in ((0, 2), (1, 0)):
            recv(w1(xk(2), yk(-q), h), r_wb.at[0, q, k])
            recv(w2(xk(-q), yk(2), h), r_wb.at[1, q, k])
    for k in range(1, NYT):
        recv(w3(yk(-k)), r_wa.at[2, k])

    def halo_wait():
        @pl.when(x > 0)
        def _():
            recv(X.at[1 - c, 0], r_xf.at[0])

        @pl.when(x < NXT - 1)
        def _():
            recv(X.at[1 - c, 6], r_xf.at[1])

    bias = wt[x, 7].astype(F32)[:, 0:1]
    lane = lax.broadcasted_iota(jnp.int32, (half, 128), 1)

    def compute(p):
        acc = None
        for a in range(3):
            for bq in range(3):
                t = 9 * a + 3 * bq
                lhs = jnp.concatenate([wt[tap_slot(t + q)] for q in range(3)], axis=0)
                rhs = jnp.concatenate(
                    [
                        jnp.concatenate([X[0, p + a, r + bq], X[1, p + a, r + bq]], axis=0)
                        for r in range(2)
                    ],
                    axis=1,
                )
                part = jnp.dot(lhs, rhs, preferred_element_type=F32)
                acc = part if acc is None else acc + part
        for r in range(2):
            cols = acc[:, 128 * r:128 * r + 128]
            low = jnp.where(lane == 0, 0.0, pltpu.roll(cols[0:half], 1, 1))
            high = jnp.where(lane == 127, 0.0, pltpu.roll(cols[2 * half:], 127, 1))
            total = low + cols[half:2 * half] + high + bias
            O[p, r] = jnp.where(total > 0, total, 0.3 * total).astype(BF16)

    def out_y(p):
        for k in (2, 1, 3):
            d = yk(k)
            sent.append(
                send(
                    O.at[p, :, pl.ds(pl.multiple_of(d * blk, blk), blk), :],
                    oy.at[p, pl.ds(2 * y, 2)],
                    s_oy.at[p, k], r_oy.at[p, k], at(z, d, c, x),
                )
            )
        oy[p, pl.ds(2 * y, 2)] = O[p, :, pl.ds(yoff, blk), :]

    def out_z(p):
        for k in range(1, NYT):
            recv(oy.at[p, pl.ds(2 * yk(-k), 2)], r_oy.at[p, k])
        for r in range(8):
            fo[p, blk * r:blk * r + blk, :] = oy[p, r].astype(F32)
        for m in range(blk):
            oz[p, m // 4, m % 4] = fo[p, pl.ds(m, 8, stride=blk), :].astype(BF16)
        for k in z_order:
            d = zk(k)
            sent.append(
                send(oz.at[p, d], out.at[:, p, z], s_oz.at[p, k], r_oz.at[p, k], at(d, y, c, x))
            )
        return local(oz.at[p, z], out.at[:, p, z], loc_p.at[10 + p])

    finals = []
    order = [1, 2, 3, 0, 4]
    for n, p in enumerate(order):
        if n == 3:
            halo_wait()
        compute(p)
        out_y(p)
        if n >= OUT_LAG:
            finals.append(out_z(order[n - OUT_LAG]))
    for p in order[5 - OUT_LAG:]:
        finals.append(out_z(p))

    for cp in finals:
        cp.wait()
    for p in order:
        for k in range(1, nz):
            recv(out.at[:, p, zk(-k)], r_oz.at[p, k])
    for cp in sent:
        cp.wait_send()

    @pl.when(x < NXT - 1)
    def _():
        recv(X.at[c, 5], s_xh.at[0])
        recv(X.at[c, 6], s_xf.at[1])

    @pl.when(x > 0)
    def _():
        recv(X.at[c, 1], s_xh.at[1])
        recv(X.at[c, 0], s_xf.at[0])


def shards(nz, volume, weight, channel_bias):
    blk = 4 * nz
    half = NYT * blk
    n_in = 2 * half
    v = volume.reshape(4, 5, nz, 8, 128)
    w = weight.transpose(1, 0, 2)
    b = channel_bias.reshape(1, 4)
    vm = pltpu.VMEM
    dma = pltpu.SemaphoreType.DMA
    out = pl.pallas_call(
        functools.partial(kernel, nz),
        out_shape=pltpu.VMEM((4, 5, nz, 8, 128), BF16),
        in_specs=[pl.BlockSpec(memory_space=pl.ANY)] * 3,
        out_specs=pl.BlockSpec(memory_space=pltpu.VMEM),
        scratch_shapes=[
            vm((1, 4), BF16),
            vm((5, nz, 5, 8, 128), BF16),
            vm((5, blk * 8, 128), F32),
            vm((5, nz, 8, 128), F32),
            vm((5, nz, 5, 8, 128), BF16),
            vm((5, blk * 8, 128), F32),
            vm((10, blk, 128), F32),
            vm((5, 10, blk, 128), BF16),
            vm((2, 7, 4, half, 128), BF16),
            vm((8, 4, n_in), BF16),
            vm((nz, 8, 4, n_in), BF16),
            vm((8, blk, n_in), F32),
            vm((4, 8, half, n_in), BF16),
            vm((5, 2, half, 128), BF16),
            vm((5, 8, blk, 128), BF16),
            vm((5, 8 * blk, 128), F32),
            vm((5, nz, 4, 8, 128), BF16),
            dma((5, nz)), dma((5, nz)), dma((nz,)), dma((nz,)),
            dma((3, 4)), dma((3, 4)), dma((2, 4, 4)), dma((2, 4, 4)),
            dma((5, 4)), dma((5, 4)), dma((5,)), dma((5,)), dma((2,)), dma((2,)), dma((2,)), dma((2,)),
            dma((5, 4)), dma((5, 4)), dma((5, nz)), dma((5, nz)), dma((5,)), dma((19,)),
        ],
        compiler_params=pltpu.CompilerParams(
            collective_id=0, has_side_effects=True, vmem_limit_bytes=56 * 1024 * 1024
        ),
        cost_estimate=pl.CostEstimate(
            flops=2 * 640 * n_in * n_in * 27, bytes_accessed=2 * v.size * 2, transcendentals=0
        ),
    )(v, w, b)
    return out.reshape(volume.shape)


def solution(mesh):
    nz = mesh.shape["ch"] // (2 * NYT)
    return jax.shard_map(
        functools.partial(shards, nz),
        mesh=mesh,
        in_specs=(P("ch", "sp", None, None), P("ch", None, None), P("ch")),
        out_specs=P("ch", "sp", None, None),
        check_vma=False,
    )
```

```python
import functools

import jax
import jax.numpy as jnp
from jax import lax
from jax.experimental import pallas as pl
from jax.experimental.pallas import tpu as pltpu
from jax.sharding import PartitionSpec as P

NYT = 4
NXT = 4
PLANES = (4, 0, 1, 2, 3)
OUT_LAG = 3
N1 = 5
STEPS = ("v4", "v0", "f1", "f3", "g0", "v1", "f2", "v2", "v3", "g1", "g3", "c4", "c0", "g2", "c1", "c2", "c3", "h")
MESH = pl.DeviceIdType.MESH
F32 = jnp.float32
BF16 = jnp.bfloat16


def tap_slot(t):
    return (t // 7, t % 7) if t <= 20 else (3, t - 20)


def kernel(
    nz, v_hbm, w_hbm, b_hbm, out,
    b, va, fe, et, rz, f, g2, xz, X, ws, wz, wf, wt, O, oy, fo, oz,
    s_vz, r_vz, s_wz, r_wz, s_wa, r_wa, s_w3, r_w3, s_wb, r_wb, r_wh,
    s_xy, r_xy, s_cc, r_cc, s_xh, r_xh, s_xf, r_xf, s_oy, r_oy, s_oz, r_oz, loc,
):
    blk = 4 * nz
    half = NYT * blk
    ch = lax.axis_index("ch")
    x = lax.axis_index("sp")
    c = lax.rem(ch, 2)
    y = lax.rem(lax.div(ch, 2), NYT)
    z = lax.div(ch, 2 * NYT)

    def at(zz, yy, cc, xx):
        return {"ch": (zz * NYT + yy) * 2 + cc, "sp": xx}

    def zk(k):
        return lax.rem(z + k + nz, nz)

    def yk(k):
        return lax.rem(y + k + NYT, NYT)

    xl, xr = lax.rem(x + NXT - 1, NXT), lax.rem(x + 1, NXT)
    sib = at(z, y, 1 - c, x)
    right, left = at(z, y, c, xr), at(z, y, c, xl)

    def send(src, dst, ss, rs, to):
        cp = pltpu.make_async_remote_copy(
            src_ref=src, dst_ref=dst, send_sem=ss, recv_sem=rs, device_id=to, device_id_type=MESH
        )
        cp.start()
        return cp

    def recv(dst, sem):
        pltpu.make_async_copy(dst, dst, sem).wait()

    def local(src, dst, sem):
        cp = pltpu.make_async_copy(src, dst, sem)
        cp.start()
        return cp

    z_order = sorted(range(1, nz), key=lambda k: -min(k, nz - k))

    bar = pltpu.get_barrier_semaphore()
    peers = [at(zk(k), y, c, x) for k in range(1, nz)]
    peers += [at(z, yk(k), c, x) for k in range(1, NYT)]
    peers += [at(z, y, c, lax.rem(x + k, NXT)) for k in range(1, NXT)]
    peers += [sib]
    start = jnp.minimum(7 * x, 20)
    loads = [
        local(w_hbm.at[pl.ds(start, 7)], ws.at[pl.ds(0, 7)], loc.at[0]),
        local(b_hbm, b, loc.at[1]),
    ]
    for j in range(4):
        local(v_hbm.at[j], va.at[:, :, j], loc.at[2])
    for p in peers:
        pl.semaphore_signal(bar, inc=1, device_id=p, device_id_type=MESH)

    @pl.when(x == 0)
    def _():
        X[:, 0] = jnp.zeros_like(X[:, 0])

    @pl.when(x == NXT - 1)
    def _():
        X[:, 6] = jnp.zeros_like(X[:, 6])

    n_in = 2 * half
    i = lax.broadcasted_iota(jnp.int32, (n_in, n_in), 0)
    o = lax.broadcasted_iota(jnp.int32, (n_in, n_in), 1)
    to = ((i >> 2) & 1) * half + ((i >> 3) & 3) * blk + (i >> 5) * 4 + (i & 3)
    perm = jnp.where(to == o, 1.0, 0.0).astype(BF16)

    loads[1].wait()
    bb = jnp.broadcast_to(b[...].astype(F32), (4, 4))
    eye = lax.broadcasted_iota(jnp.int32, (4, 4), 0) == lax.broadcasted_iota(jnp.int32, (4, 4), 1)
    col = jnp.sum(jnp.where(eye, bb, 0.0), axis=1, keepdims=True)
    ws[7] = jnp.broadcast_to(col, ws.shape[1:]).astype(BF16)

    loads[0].wait()

    pl.semaphore_wait(bar, len(peers))

    for k in z_order:
        send(ws, wz.at[z], s_wz, r_wz, at(zk(k), y, c, x))
    local(ws, wz.at[z], r_wz)
    recv(va.at[:, :, pl.ds(0, 4)], loc.at[2])
    for p in PLANES:
        for d in range(nz):
            for j in range(4):
                r0 = (d * 4 + j) * 8
                fe[p, r0:r0 + 8, :] = va[p, d, j].astype(F32)
        for d in range(nz):
            et[p, d, 0:4, :] = (
                fe[p, pl.ds((d - 1) * 32 + 7, 4, stride=8), :] if d else jnp.zeros((4, 128), F32)
            )
            et[p, d, 4:8, :] = (
                fe[p, pl.ds((d + 1) * 32, 4, stride=8), :] if d < nz - 1 else jnp.zeros((4, 128), F32)
            )
            va[p, d, 4] = et[p, d].astype(BF16)
        for k in z_order:
            d = zk(k)
            send(
                *(va.at[p, d], rz.at[p, z], s_vz, r_vz.at[p], at(d, y, c, x))
            )
        local(va.at[p, z], rz.at[p, z], r_vz.at[p])

    recv(wz, r_wz)
    for t in range(8):
        for s in range(nz):
            wf[t, 4 * s:4 * s + 4, :] = wz[s, t].astype(F32)
    yoff = pl.multiple_of(y * blk, blk)
    for t in range(8):
        wt[x, t, pl.ds(yoff, blk), :] = jnp.dot(
            wf[t].astype(BF16), perm, preferred_element_type=F32
        ).astype(BF16)

    def rows(yy):
        return pl.ds(pl.multiple_of(yy * blk, blk), blk)

    def part_rows(yy, h):
        if h is None:
            return rows(yy)
        return pl.ds(pl.multiple_of(yy * blk + h * (blk // 2), blk // 2), blk // 2)

    def w1(g, yy, h=None):
        return wt.at[g, pl.ds(0, N1), part_rows(yy, h), :]

    def w2(g, yy, h=None):
        return wt.at[g, pl.ds(N1, 7 - N1), part_rows(yy, h), :]

    def w3(yy):
        return wt.at[x, 7, rows(yy), pl.ds(0, min(128, n_in))]

    def xk(k):
        return lax.rem(x + k + NXT, NXT)

    for k in (1, 3, 2):
        send(w1(x, y), w1(x, y), s_wa, r_wa.at[0, k - 1], at(z, yk(k), c, x))
        send(w2(x, y), w2(x, y), s_wa, r_wa.at[1, k - 1], at(z, y, c, xk(k)))
        send(w3(y), w3(y), s_w3, r_w3, at(z, yk(k), c, x))

    def forward(q):
        yq, xq = yk(-q), xk(-q)
        if q:
            recv(w1(x, yq), r_wa.at[0, q - 1])
        for k in (1, 3):
            to = at(z, y, c, xk(k))
            send(w1(x, yq), w1(x, yq), s_wb, r_wb.at[0, q, k // 2], to)
        if q:
            recv(w2(xq, y), r_wa.at[1, q - 1])
        for k in (1, 3):
            to = at(z, yk(k), c, x)
            send(w2(xq, y), w2(xq, y), s_wb, r_wb.at[1, q, k // 2], to)

    def pass_on(q):
        yq, xq = yk(-q), xk(-q)
        recv(w1(xk(-1), yq), r_wb.at[0, q, 0])
        half0 = w1(xk(-1), yq, 0)
        send(half0, half0, s_wb, r_wh, at(z, y, c, xk(1)))
        recv(w1(xk(1), yq), r_wb.at[0, q, 1])
        half1 = w1(xk(1), yq, 1)
        send(half1, half1, s_wb, r_wh, at(z, y, c, xk(-1)))
        recv(w2(xq, yk(-1)), r_wb.at[1, q, 0])
        half2 = w2(xq, yk(-1), 0)
        send(half2, half2, s_wb, r_wh, at(z, yk(1), c, x))
        recv(w2(xq, yk(1)), r_wb.at[1, q, 1])
        half3 = w2(xq, yk(1), 1)
        send(half3, half3, s_wb, r_wh, at(z, yk(-1), c, x))

    forward(0)

    def x_part(p, yy):
        return X.at[c, p + 1, :, pl.ds(pl.multiple_of(yy * blk, blk), blk), :]

    def volume_y(p):
        recv(rz.at[p], r_vz.at[p])
        for s in range(nz):
            for j in range(4):
                r0 = (s * 4 + j) * 8
                f[p, r0:r0 + 8, :] = rz[p, s, j].astype(F32)
        for s in range(nz):
            e = rz[p, s, 4].astype(F32)
            g2[p, 4 * s:4 * s + 4, :] = e[0:4]
            g2[5 + p, 4 * s:4 * s + 4, :] = e[4:8]
        xz[p, 0] = g2[p].astype(BF16)
        xz[p, 9] = g2[5 + p].astype(BF16)
        for r in range(8):
            xz[p, r + 1] = f[p, pl.ds(r, blk, stride=8), :].astype(BF16)
        for k in (2, 1, 3):
            d = yk(k)
            send(
                *(
                    xz.at[p, pl.ds(2 * d, 4)], x_part(p, y), s_xy, r_xy.at[p],
                    at(z, d, c, x),
                )
            )
        local(xz.at[p, pl.ds(2 * y, 4)], x_part(p, y), r_xy.at[p])

    def share(p):
        recv(X.at[c, p + 1], r_xy.at[p])
        if p == 4:
            @pl.when(x < NXT - 1)
            def _():
                send(X.at[c, 5], X.at[c, 0], s_xh.at[0], r_xh.at[0], right)
        if p == 0:
            @pl.when(x > 0)
            def _():
                send(X.at[c, 1], X.at[c, 6], s_xh.at[1], r_xh.at[1], left)
        send(X.at[c, p + 1], X.at[c, p + 1], s_cc, r_cc, sib)

    def halo():
        @pl.when(x > 0)
        def _():
            recv(X.at[c, 0], r_xh.at[0])
            send(X.at[c, 0], X.at[c, 0], s_xf.at[0], r_xf.at[0], sib)

        @pl.when(x < NXT - 1)
        def _():
            recv(X.at[c, 6], r_xh.at[1])
            send(X.at[c, 6], X.at[c, 6], s_xf.at[1], r_xf.at[1], sib)

    for step in STEPS:
        if step[0] == "v":
            volume_y(int(step[1]))
        elif step[0] == "f":
            forward(int(step[1]))
        elif step[0] == "g":
            pass_on(int(step[1]))
        elif step[0] == "c":
            share(int(step[1]))
        else:
            halo()

    recv(X.at[1 - c, pl.ds(1, 5)], r_cc)

    recv(wt.at[0, pl.ds(0, 7)], r_wh)
    recv(wt.at[pl.ds(0, 3), 7, rows(y), pl.ds(0, min(128, n_in))], r_w3)

    def halo_wait():
        @pl.when(x > 0)
        def _():
            recv(X.at[1 - c, 0], r_xf.at[0])

        @pl.when(x < NXT - 1)
        def _():
            recv(X.at[1 - c, 6], r_xf.at[1])

    bias = wt[x, 7].astype(F32)[:, 0:1]
    lane = lax.broadcasted_iota(jnp.int32, (half, 128), 1)

    def compute(p):
        acc = None
        for a in range(3):
            for bq in range(3):
                t = 9 * a + 3 * bq
                lhs = jnp.concatenate([wt[tap_slot(t + q)] for q in range(3)], axis=0)
                rhs = jnp.concatenate(
                    [
                        jnp.concatenate([X[0, p + a, r + bq], X[1, p + a, r + bq]], axis=0)
                        for r in range(2)
                    ],
                    axis=1,
                )
                part = jnp.dot(lhs, rhs, preferred_element_type=F32)
                acc = part if acc is None else acc + part
        for r in range(2):
            cols = acc[:, 128 * r:128 * r + 128]
            low = jnp.where(lane == 0, 0.0, pltpu.roll(cols[0:half], 1, 1))
            high = jnp.where(lane == 127, 0.0, pltpu.roll(cols[2 * half:], 127, 1))
            total = low + cols[half:2 * half] + high + bias
            O[p, r] = jnp.where(total > 0, total, 0.3 * total).astype(BF16)

    def out_y(p):
        for k in (2, 1, 3):
            d = yk(k)
            send(
                *(
                    O.at[p, :, pl.ds(pl.multiple_of(d * blk, blk), blk), :],
                    oy.at[p, pl.ds(2 * y, 2)],
                    s_oy, r_oy.at[p], at(z, d, c, x),
                )
            )
        oy[p, pl.ds(2 * y, 2)] = O[p, :, pl.ds(yoff, blk), :]

    def out_z(p):
        recv(oy.at[p, pl.ds(0, 6)], r_oy.at[p])
        for r in range(8):
            fo[p, blk * r:blk * r + blk, :] = oy[p, r].astype(F32)
        for m in range(blk):
            oz[p, m // 4, m % 4] = fo[p, pl.ds(m, 8, stride=blk), :].astype(BF16)
        for k in z_order:
            d = zk(k)
            send(
                *(oz.at[p, d], out.at[:, p, z], s_oz, r_oz, at(d, y, c, x))
            )
        local(oz.at[p, z], out.at[:, p, z], r_oz)

    order = [1, 2, 3, 0, 4]
    for n, p in enumerate(order):
        if n == 3:
            halo_wait()
        compute(p)
        out_y(p)
        if n >= OUT_LAG:
            out_z(order[n - OUT_LAG])
    for p in order[5 - OUT_LAG:]:
        out_z(p)

    recv(out, r_oz)
    recv(wz.at[pl.ds(0, nz - 1)], s_wz)
    recv(rz.at[:, pl.ds(0, nz - 1)], s_vz)
    recv(wt.at[pl.ds(0, 3), pl.ds(0, 7), rows(y), :], s_wa)
    recv(wt.at[pl.ds(0, 3), 7, rows(y), pl.ds(0, min(128, n_in))], s_w3)
    recv(wt.at[pl.ds(0, 3), pl.ds(0, 7)], s_wb)
    recv(X.at[0, pl.ds(0, 5), :, pl.ds(0, 3 * blk), :], s_xy)
    recv(X.at[0, pl.ds(1, 5)], s_cc)
    recv(O.at[:, :, pl.ds(0, 3 * blk), :], s_oy)
    recv(oz.at[:, pl.ds(0, nz - 1)], s_oz)

    @pl.when(x < NXT - 1)
    def _():
        recv(X.at[c, 5], s_xh.at[0])
        recv(X.at[c, 6], s_xf.at[1])

    @pl.when(x > 0)
    def _():
        recv(X.at[c, 1], s_xh.at[1])
        recv(X.at[c, 0], s_xf.at[0])


def shards(nz, volume, weight, channel_bias):
    blk = 4 * nz
    half = NYT * blk
    n_in = 2 * half
    v = volume.reshape(4, 5, nz, 8, 128)
    w = weight.transpose(1, 0, 2)
    b = channel_bias.reshape(1, 4)
    vm = pltpu.VMEM
    dma = pltpu.SemaphoreType.DMA
    out = pl.pallas_call(
        functools.partial(kernel, nz),
        out_shape=pltpu.VMEM((4, 5, nz, 8, 128), BF16),
        in_specs=[pl.BlockSpec(memory_space=pl.ANY)] * 3,
        out_specs=pl.BlockSpec(memory_space=pltpu.VMEM),
        scratch_shapes=[
            vm((1, 4), BF16),
            vm((5, nz, 5, 8, 128), BF16),
            vm((5, blk * 8, 128), F32),
            vm((5, nz, 8, 128), F32),
            vm((5, nz, 5, 8, 128), BF16),
            vm((5, blk * 8, 128), F32),
            vm((10, blk, 128), F32),
            vm((5, 10, blk, 128), BF16),
            vm((2, 7, 4, half, 128), BF16),
            vm((8, 4, n_in), BF16),
            vm((nz, 8, 4, n_in), BF16),
            vm((8, blk, n_in), F32),
            vm((4, 8, half, n_in), BF16),
            vm((5, 2, half, 128), BF16),
            vm((5, 8, blk, 128), BF16),
            vm((5, 8 * blk, 128), F32),
            vm((5, nz, 4, 8, 128), BF16),
            dma(()), dma((5,)), dma(()), dma(()),
            dma(()), dma((2, 3)), dma(()), dma(()), dma(()), dma((2, 4, 2)), dma(()),
            dma(()), dma((5,)), dma(()), dma(()), dma((2,)), dma((2,)), dma((2,)), dma((2,)),
            dma(()), dma((5,)), dma(()), dma(()), dma((3,)),
        ],
        compiler_params=pltpu.CompilerParams(
            collective_id=0, has_side_effects=True, vmem_limit_bytes=56 * 1024 * 1024
        ),
        cost_estimate=pl.CostEstimate(
            flops=2 * 640 * n_in * n_in * 27, bytes_accessed=2 * v.size * 2, transcendentals=0
        ),
    )(v, w, b)
    return out.reshape(volume.shape)


def solution(mesh):
    nz = mesh.shape["ch"] // (2 * NYT)
    return jax.shard_map(
        functools.partial(shards, nz),
        mesh=mesh,
        in_specs=(P("ch", "sp", None, None), P("ch", None, None), P("ch")),
        out_specs=P("ch", "sp", None, None),
        check_vma=False,
    )
```

```python
import functools

import jax
import jax.numpy as jnp
from jax import lax
from jax.experimental import pallas as pl
from jax.experimental.pallas import tpu as pltpu
from jax.sharding import PartitionSpec as P

NYT = 4
NXT = 4
PLANES = (4, 0, 1, 2, 3)
N1 = 5
STEPS = ("v4", "v0", "f1", "f3", "g0", "v1", "f2", "v2", "v3", "g1", "g3", "c4", "c0", "g2", "c1", "c2", "c3", "h")
MESH = pl.DeviceIdType.MESH
F32 = jnp.float32
BF16 = jnp.bfloat16


def tap_slot(t):
    return (t // 7, t % 7) if t <= 20 else (3, t - 20)


def kernel(
    nz, v_hbm, w_hbm, b_hbm, out,
    b, va, fe, et, rz, f, g2, xz, X, ws, wz, wf, wt, O, oy, fo, oz, fz, oz1, iz, fy, oy1, iy, fl,
    s_vz, r_vz, s_wz, r_wz, s_wa, r_wa, s_w3, r_w3, s_wb, r_wb, r_wh,
    s_xy, r_xy, s_cc, r_cc, s_xh, r_xh, s_xf, r_xf, s_oy, r_oy, s_oz, r_oz, s_z1, r_z1, s_y1, r_y1, loc,
):
    blk = 4 * nz
    half = NYT * blk
    ch = lax.axis_index("ch")
    x = lax.axis_index("sp")
    c = lax.rem(ch, 2)
    y = lax.rem(lax.div(ch, 2), NYT)
    z = lax.div(ch, 2 * NYT)

    def at(zz, yy, cc, xx):
        return {"ch": (zz * NYT + yy) * 2 + cc, "sp": xx}

    def zk(k):
        return lax.rem(z + k + nz, nz)

    def yk(k):
        return lax.rem(y + k + NYT, NYT)

    xl, xr = lax.rem(x + NXT - 1, NXT), lax.rem(x + 1, NXT)
    sib = at(z, y, 1 - c, x)
    right, left = at(z, y, c, xr), at(z, y, c, xl)

    def send(src, dst, ss, rs, to):
        cp = pltpu.make_async_remote_copy(
            src_ref=src, dst_ref=dst, send_sem=ss, recv_sem=rs, device_id=to, device_id_type=MESH
        )
        cp.start()
        return cp

    def recv(dst, sem):
        pltpu.make_async_copy(dst, dst, sem).wait()

    def local(src, dst, sem):
        cp = pltpu.make_async_copy(src, dst, sem)
        cp.start()
        return cp

    z_order = sorted(range(1, nz), key=lambda k: -min(k, nz - k))

    bar = pltpu.get_barrier_semaphore()
    peers = [at(zk(k), y, c, x) for k in range(1, nz)]
    peers += [at(z, yk(k), c, x) for k in range(1, NYT)]
    peers += [at(z, y, c, lax.rem(x + k, NXT)) for k in range(1, NXT)]
    peers += [sib]
    start = jnp.minimum(7 * x, 20)
    loads = [
        local(w_hbm.at[pl.ds(start, 7)], ws.at[pl.ds(0, 7)], loc.at[0]),
        local(b_hbm, b, loc.at[1]),
    ]
    for j in range(4):
        local(v_hbm.at[j], va.at[:, :, j], loc.at[2])
    for p in peers:
        pl.semaphore_signal(bar, inc=1, device_id=p, device_id_type=MESH)

    @pl.when(x == 0)
    def _():
        X[:, 0] = jnp.zeros_like(X[:, 0])

    @pl.when(x == NXT - 1)
    def _():
        X[:, 6] = jnp.zeros_like(X[:, 6])

    n_in = 2 * half
    i = lax.broadcasted_iota(jnp.int32, (n_in, n_in), 0)
    o = lax.broadcasted_iota(jnp.int32, (n_in, n_in), 1)
    to = ((i >> 2) & 1) * half + ((i >> 3) & 3) * blk + (i >> 5) * 4 + (i & 3)
    perm = jnp.where(to == o, 1.0, 0.0).astype(BF16)

    loads[1].wait()
    bb = jnp.broadcast_to(b[...].astype(F32), (4, 4))
    eye = lax.broadcasted_iota(jnp.int32, (4, 4), 0) == lax.broadcasted_iota(jnp.int32, (4, 4), 1)
    col = jnp.sum(jnp.where(eye, bb, 0.0), axis=1, keepdims=True)
    ws[7] = jnp.broadcast_to(col, ws.shape[1:]).astype(BF16)

    loads[0].wait()

    pl.semaphore_wait(bar, len(peers))

    for k in z_order:
        send(ws, wz.at[z], s_wz, r_wz, at(zk(k), y, c, x))
    local(ws, wz.at[z], r_wz)
    recv(va.at[:, :, pl.ds(0, 4)], loc.at[2])
    for p in PLANES:
        for d in range(nz):
            for j in range(4):
                r0 = (d * 4 + j) * 8
                fe[p, r0:r0 + 8, :] = va[p, d, j].astype(F32)
        for d in range(nz):
            et[p, d, 0:4, :] = (
                fe[p, pl.ds((d - 1) * 32 + 7, 4, stride=8), :] if d else jnp.zeros((4, 128), F32)
            )
            et[p, d, 4:8, :] = (
                fe[p, pl.ds((d + 1) * 32, 4, stride=8), :] if d < nz - 1 else jnp.zeros((4, 128), F32)
            )
            va[p, d, 4] = et[p, d].astype(BF16)
        for k in z_order:
            d = zk(k)
            send(
                *(va.at[p, d], rz.at[p, z], s_vz, r_vz.at[p], at(d, y, c, x))
            )
        local(va.at[p, z], rz.at[p, z], r_vz.at[p])

    recv(wz, r_wz)
    for t in range(8):
        for s in range(nz):
            wf[t, 4 * s:4 * s + 4, :] = wz[s, t].astype(F32)
    yoff = pl.multiple_of(y * blk, blk)
    for t in range(8):
        wt[x, t, pl.ds(yoff, blk), :] = jnp.dot(
            wf[t].astype(BF16), perm, preferred_element_type=F32
        ).astype(BF16)

    def rows(yy):
        return pl.ds(pl.multiple_of(yy * blk, blk), blk)

    def part_rows(yy, h):
        if h is None:
            return rows(yy)
        return pl.ds(pl.multiple_of(yy * blk + h * (blk // 2), blk // 2), blk // 2)

    def w1(g, yy, h=None):
        return wt.at[g, pl.ds(0, N1), part_rows(yy, h), :]

    def w2(g, yy, h=None):
        return wt.at[g, pl.ds(N1, 7 - N1), part_rows(yy, h), :]

    def w3(yy):
        return wt.at[x, 7, rows(yy), pl.ds(0, min(128, n_in))]

    def xk(k):
        return lax.rem(x + k + NXT, NXT)

    for k in (1, 3, 2):
        send(w1(x, y), w1(x, y), s_wa, r_wa.at[0, k - 1], at(z, yk(k), c, x))
        send(w2(x, y), w2(x, y), s_wa, r_wa.at[1, k - 1], at(z, y, c, xk(k)))
        send(w3(y), w3(y), s_w3, r_w3, at(z, yk(k), c, x))

    def forward(q):
        yq, xq = yk(-q), xk(-q)
        if q:
            recv(w1(x, yq), r_wa.at[0, q - 1])
        for k in (1, 3):
            to = at(z, y, c, xk(k))
            send(w1(x, yq), w1(x, yq), s_wb, r_wb.at[0, q, k // 2], to)
        if q:
            recv(w2(xq, y), r_wa.at[1, q - 1])
        for k in (1, 3):
            to = at(z, yk(k), c, x)
            send(w2(xq, y), w2(xq, y), s_wb, r_wb.at[1, q, k // 2], to)

    def pass_on(q):
        yq, xq = yk(-q), xk(-q)
        recv(w1(xk(-1), yq), r_wb.at[0, q, 0])
        half0 = w1(xk(-1), yq, 0)
        send(half0, half0, s_wb, r_wh, at(z, y, c, xk(1)))
        recv(w1(xk(1), yq), r_wb.at[0, q, 1])
        half1 = w1(xk(1), yq, 1)
        send(half1, half1, s_wb, r_wh, at(z, y, c, xk(-1)))
        recv(w2(xq, yk(-1)), r_wb.at[1, q, 0])
        half2 = w2(xq, yk(-1), 0)
        send(half2, half2, s_wb, r_wh, at(z, yk(1), c, x))
        recv(w2(xq, yk(1)), r_wb.at[1, q, 1])
        half3 = w2(xq, yk(1), 1)
        send(half3, half3, s_wb, r_wh, at(z, yk(-1), c, x))

    forward(0)

    def x_part(p, yy):
        return X.at[c, p + 1, :, pl.ds(pl.multiple_of(yy * blk, blk), blk), :]

    def volume_y(p):
        recv(rz.at[p], r_vz.at[p])
        for s in range(nz):
            for j in range(4):
                r0 = (s * 4 + j) * 8
                f[p, r0:r0 + 8, :] = rz[p, s, j].astype(F32)
        for s in range(nz):
            e = rz[p, s, 4].astype(F32)
            g2[p, 4 * s:4 * s + 4, :] = e[0:4]
            g2[5 + p, 4 * s:4 * s + 4, :] = e[4:8]
        xz[p, 0] = g2[p].astype(BF16)
        xz[p, 9] = g2[5 + p].astype(BF16)
        for r in range(8):
            xz[p, r + 1] = f[p, pl.ds(r, blk, stride=8), :].astype(BF16)
        for k in (2, 1, 3):
            d = yk(k)
            send(
                *(
                    xz.at[p, pl.ds(2 * d, 4)], x_part(p, y), s_xy, r_xy.at[p],
                    at(z, d, c, x),
                )
            )
        local(xz.at[p, pl.ds(2 * y, 4)], x_part(p, y), r_xy.at[p])

    def share(p):
        recv(X.at[c, p + 1], r_xy.at[p])
        if p == 4:
            @pl.when(x < NXT - 1)
            def _():
                send(X.at[c, 5], X.at[c, 0], s_xh.at[0], r_xh.at[0], right)
        if p == 0:
            @pl.when(x > 0)
            def _():
                send(X.at[c, 1], X.at[c, 6], s_xh.at[1], r_xh.at[1], left)
        send(X.at[c, p + 1], X.at[c, p + 1], s_cc, r_cc, sib)

    def halo():
        @pl.when(x > 0)
        def _():
            recv(X.at[c, 0], r_xh.at[0])
            send(X.at[c, 0], X.at[c, 0], s_xf.at[0], r_xf.at[0], sib)

        @pl.when(x < NXT - 1)
        def _():
            recv(X.at[c, 6], r_xh.at[1])
            send(X.at[c, 6], X.at[c, 6], s_xf.at[1], r_xf.at[1], sib)

    for step in STEPS:
        if step[0] == "v":
            volume_y(int(step[1]))
        elif step[0] == "f":
            forward(int(step[1]))
        elif step[0] == "g":
            pass_on(int(step[1]))
        elif step[0] == "c":
            share(int(step[1]))
        else:
            halo()

    recv(X.at[1 - c, pl.ds(1, 5)], r_cc)

    recv(wt.at[0, pl.ds(0, 7)], r_wh)
    recv(wt.at[pl.ds(0, 3), 7, rows(y), pl.ds(0, min(128, n_in))], r_w3)

    def halo_wait():
        @pl.when(x > 0)
        def _():
            recv(X.at[1 - c, 0], r_xf.at[0])

        @pl.when(x < NXT - 1)
        def _():
            recv(X.at[1 - c, 6], r_xf.at[1])

    bias = wt[x, 7].astype(F32)[:, 0:1]
    lane = lax.broadcasted_iota(jnp.int32, (half, 128), 1)

    def compute(p):
        acc = None
        for a in range(3):
            for bq in range(3):
                t = 9 * a + 3 * bq
                lhs = jnp.concatenate([wt[tap_slot(t + q)] for q in range(3)], axis=0)
                rhs = jnp.concatenate(
                    [
                        jnp.concatenate([X[0, p + a, r + bq], X[1, p + a, r + bq]], axis=0)
                        for r in range(2)
                    ],
                    axis=1,
                )
                part = jnp.dot(lhs, rhs, preferred_element_type=F32)
                acc = part if acc is None else acc + part
        for r in range(2):
            cols = acc[:, 128 * r:128 * r + 128]
            low = jnp.where(lane == 0, 0.0, pltpu.roll(cols[0:half], 1, 1))
            high = jnp.where(lane == 127, 0.0, pltpu.roll(cols[2 * half:], 127, 1))
            total = low + cols[half:2 * half] + high + bias
            O[p, r] = jnp.where(total > 0, total, 0.3 * total).astype(BF16)

    def out_y(p):
        for k in (2, 1, 3):
            d = yk(k)
            send(
                *(
                    O.at[p, :, pl.ds(pl.multiple_of(d * blk, blk), blk), :],
                    oy.at[p, pl.ds(2 * y, 2)],
                    s_oy, r_oy.at[p], at(z, d, c, x),
                )
            )
        oy[p, pl.ds(2 * y, 2)] = O[p, :, pl.ds(yoff, blk), :]

    def out_z(p):
        recv(oy.at[p, pl.ds(0, 6)], r_oy.at[p])
        for r in range(8):
            fo[p, blk * r:blk * r + blk, :] = oy[p, r].astype(F32)
        for m in range(blk):
            oz[p, m // 4, m % 4] = fo[p, pl.ds(m, 8, stride=blk), :].astype(BF16)
        for k in z_order:
            d = zk(k)
            send(
                *(oz.at[p, d], out.at[:, p, z], s_oz, r_oz, at(d, y, c, x))
            )
        local(oz.at[p, z], out.at[:, p, z], r_oz)

    def first_z(p, i):
        for r in range(2):
            fo[p, half * r:half * r + half, :] = O[p, r].astype(F32)
            for zz in range(nz):
                for yy in range(NYT):
                    r0 = half * r + blk * yy + 4 * zz
                    fz[i, zz, r, 4 * yy:4 * yy + 4, :] = fo[p, r0:r0 + 4, :]
                oz1[i, zz, r] = fz[i, zz, r].astype(BF16)
        for k in z_order:
            d = zk(k)
            send(oz1.at[i, d], iz.at[i, z], s_z1, r_z1.at[i], at(d, y, c, x))
        local(oz1.at[i, z], iz.at[i, z], r_z1.at[i])

    def then_y(i):
        recv(iz.at[i], r_z1.at[i])
        for zz in range(nz):
            for r in range(2):
                rows16 = iz[i, zz, r].astype(F32)
                r0 = (zz * 2 + r) * 4
                for yy in range(NYT):
                    fy[i, yy, r0:r0 + 4, :] = rows16[4 * yy:4 * yy + 4]
        for yy in range(NYT):
            oy1[i, yy] = fy[i, yy].astype(BF16)
        for k in (2, 1, 3):
            d = yk(k)
            send(oy1.at[i, d], iy.at[i, y], s_y1, r_y1.at[i], at(z, d, c, x))
        local(oy1.at[i, y], iy.at[i, y], r_y1.at[i])

    def finish(p, i):
        recv(iy.at[i], r_y1.at[i])
        for yy in range(NYT):
            block = iy[i, yy].astype(F32)
            for zz in range(nz):
                fl[i, zz, 8 * yy:8 * yy + 8, :] = block[8 * zz:8 * zz + 8]
        for zz in range(nz):
            for j in range(4):
                out[j, p, zz] = fl[i, zz, pl.ds(j, 8, stride=4), :].astype(BF16)

    compute(1)
    first_z(1, 0)
    compute(2)
    first_z(2, 1)
    compute(3)
    out_y(3)
    halo_wait()
    compute(0)
    out_y(0)
    compute(4)
    out_y(4)
    then_y(0)
    out_z(3)
    then_y(1)
    out_z(0)
    out_z(4)
    finish(1, 0)
    finish(2, 1)

    recv(out.at[:, pl.ds(0, 3)], r_oz)
    recv(wz.at[pl.ds(0, nz - 1)], s_wz)
    recv(rz.at[:, pl.ds(0, nz - 1)], s_vz)
    recv(wt.at[pl.ds(0, 3), pl.ds(0, 7), rows(y), :], s_wa)
    recv(wt.at[pl.ds(0, 3), 7, rows(y), pl.ds(0, min(128, n_in))], s_w3)
    recv(wt.at[pl.ds(0, 3), pl.ds(0, 7)], s_wb)
    recv(X.at[0, pl.ds(0, 5), :, pl.ds(0, 3 * blk), :], s_xy)
    recv(X.at[0, pl.ds(1, 5)], s_cc)
    recv(O.at[pl.ds(0, 3), :, pl.ds(0, 3 * blk), :], s_oy)
    recv(oz.at[pl.ds(0, 3), pl.ds(0, nz - 1)], s_oz)
    recv(oz1.at[:, pl.ds(0, nz - 1)], s_z1)
    recv(oy1.at[:, pl.ds(0, 3)], s_y1)

    @pl.when(x < NXT - 1)
    def _():
        recv(X.at[c, 5], s_xh.at[0])
        recv(X.at[c, 6], s_xf.at[1])

    @pl.when(x > 0)
    def _():
        recv(X.at[c, 1], s_xh.at[1])
        recv(X.at[c, 0], s_xf.at[0])


def shards(nz, volume, weight, channel_bias):
    blk = 4 * nz
    half = NYT * blk
    n_in = 2 * half
    v = volume.reshape(4, 5, nz, 8, 128)
    w = weight.transpose(1, 0, 2)
    b = channel_bias.reshape(1, 4)
    vm = pltpu.VMEM
    dma = pltpu.SemaphoreType.DMA
    out = pl.pallas_call(
        functools.partial(kernel, nz),
        out_shape=pltpu.VMEM((4, 5, nz, 8, 128), BF16),
        in_specs=[pl.BlockSpec(memory_space=pl.ANY)] * 3,
        out_specs=pl.BlockSpec(memory_space=pltpu.VMEM),
        scratch_shapes=[
            vm((1, 4), BF16),
            vm((5, nz, 5, 8, 128), BF16),
            vm((5, blk * 8, 128), F32),
            vm((5, nz, 8, 128), F32),
            vm((5, nz, 5, 8, 128), BF16),
            vm((5, blk * 8, 128), F32),
            vm((10, blk, 128), F32),
            vm((5, 10, blk, 128), BF16),
            vm((2, 7, 4, half, 128), BF16),
            vm((8, 4, n_in), BF16),
            vm((nz, 8, 4, n_in), BF16),
            vm((8, blk, n_in), F32),
            vm((4, 8, half, n_in), BF16),
            vm((5, 2, half, 128), BF16),
            vm((5, 8, blk, 128), BF16),
            vm((5, 8 * blk, 128), F32),
            vm((5, nz, 4, 8, 128), BF16),
            vm((2, nz, 2, 16, 128), F32),
            vm((2, nz, 2, 16, 128), BF16),
            vm((2, nz, 2, 16, 128), BF16),
            vm((2, NYT, 8 * nz, 128), F32),
            vm((2, NYT, 8 * nz, 128), BF16),
            vm((2, NYT, 8 * nz, 128), BF16),
            vm((2, nz, 32, 128), F32),
            dma(()), dma((5,)), dma(()), dma(()),
            dma(()), dma((2, 3)), dma(()), dma(()), dma(()), dma((2, 4, 2)), dma(()),
            dma(()), dma((5,)), dma(()), dma(()), dma((2,)), dma((2,)), dma((2,)), dma((2,)),
            dma(()), dma((5,)), dma(()), dma(()), dma(()), dma((2,)), dma(()), dma((2,)), dma((3,)),
        ],
        compiler_params=pltpu.CompilerParams(
            collective_id=0, has_side_effects=True, vmem_limit_bytes=56 * 1024 * 1024
        ),
        cost_estimate=pl.CostEstimate(
            flops=2 * 640 * n_in * n_in * 27, bytes_accessed=2 * v.size * 2, transcendentals=0
        ),
    )(v, w, b)
    return out.reshape(volume.shape)


def solution(mesh):
    nz = mesh.shape["ch"] // (2 * NYT)
    return jax.shard_map(
        functools.partial(shards, nz),
        mesh=mesh,
        in_specs=(P("ch", "sp", None, None), P("ch", None, None), P("ch")),
        out_specs=P("ch", "sp", None, None),
        check_vma=False,
    )
```

```python
import functools

import jax
import jax.numpy as jnp
from jax import lax
from jax.experimental import pallas as pl
from jax.experimental.pallas import tpu as pltpu
from jax.sharding import PartitionSpec as P

NYT = 4
NXT = 4
PLANES = (4, 0, 1, 2, 3)
N1 = 5
STEPS = ("v4", "v0", "f1", "f3", "g0", "v1", "f2", "v2", "v3", "g1", "g3", "c4", "c0", "g2", "c1", "c2", "c3", "h")
MESH = pl.DeviceIdType.MESH
F32 = jnp.float32
BF16 = jnp.bfloat16


def tap_slot(t):
    return (t // 7, t % 7) if t <= 20 else (3, t - 20)


def kernel(
    nz, v_hbm, w_hbm, b_hbm, out,
    b, va, fe, et, rz, f, g2, xz, X, ws, wz, wf, wt, O, oy, fo, oz, fz, oz1, iz, fy, oy1, iy, fl,
    s_vz, r_vz, s_wz, r_wz, s_wa, r_wa, s_w3, r_w3, s_wb, r_wb, r_wh,
    s_xy, r_xy, s_cc, r_cc, s_xh, r_xh, s_xf, r_xf, s_oy, r_oy, s_oz, r_oz, s_z1, r_z1, s_y1, r_y1, loc,
):
    blk = 4 * nz
    half = NYT * blk
    ch = lax.axis_index("ch")
    x = lax.axis_index("sp")
    c = lax.rem(ch, 2)
    y = lax.rem(lax.div(ch, 2), NYT)
    z = lax.div(ch, 2 * NYT)

    def at(zz, yy, cc, xx):
        return {"ch": (zz * NYT + yy) * 2 + cc, "sp": xx}

    def zk(k):
        return lax.rem(z + k + nz, nz)

    def yk(k):
        return lax.rem(y + k + NYT, NYT)

    xl, xr = lax.rem(x + NXT - 1, NXT), lax.rem(x + 1, NXT)
    sib = at(z, y, 1 - c, x)
    right, left = at(z, y, c, xr), at(z, y, c, xl)

    def send(src, dst, ss, rs, to):
        cp = pltpu.make_async_remote_copy(
            src_ref=src, dst_ref=dst, send_sem=ss, recv_sem=rs, device_id=to, device_id_type=MESH
        )
        cp.start()
        return cp

    def recv(dst, sem):
        pltpu.make_async_copy(dst, dst, sem).wait()

    def local(src, dst, sem):
        cp = pltpu.make_async_copy(src, dst, sem)
        cp.start()
        return cp

    z_order = sorted(range(1, nz), key=lambda k: -min(k, nz - k))

    bar = pltpu.get_barrier_semaphore()
    peers = [at(zk(k), y, c, x) for k in range(1, nz)]
    peers += [at(z, yk(k), c, x) for k in range(1, NYT)]
    peers += [at(z, y, c, lax.rem(x + k, NXT)) for k in range(1, NXT)]
    peers += [sib]
    for p in peers:
        pl.semaphore_signal(bar, inc=1, device_id=p, device_id_type=MESH)
    start = jnp.minimum(7 * x, 20)
    loads = [
        local(w_hbm.at[pl.ds(start, 7)], ws.at[pl.ds(0, 7)], loc.at[0]),
        local(b_hbm, b, loc.at[1]),
    ]
    for j in range(4):
        local(v_hbm.at[j], va.at[:, :, j], loc.at[2])

    @pl.when(x == 0)
    def _():
        X[:, 0] = jnp.zeros_like(X[:, 0])

    @pl.when(x == NXT - 1)
    def _():
        X[:, 6] = jnp.zeros_like(X[:, 6])

    n_in = 2 * half
    i = lax.broadcasted_iota(jnp.int32, (n_in, n_in), 0)
    o = lax.broadcasted_iota(jnp.int32, (n_in, n_in), 1)
    to = ((i >> 2) & 1) * half + ((i >> 3) & 3) * blk + (i >> 5) * 4 + (i & 3)
    perm = jnp.where(to == o, 1.0, 0.0).astype(BF16)

    loads[1].wait()
    bb = jnp.broadcast_to(b[...].astype(F32), (4, 4))
    eye = lax.broadcasted_iota(jnp.int32, (4, 4), 0) == lax.broadcasted_iota(jnp.int32, (4, 4), 1)
    col = jnp.sum(jnp.where(eye, bb, 0.0), axis=1, keepdims=True)
    ws[7] = jnp.broadcast_to(col, ws.shape[1:]).astype(BF16)

    loads[0].wait()

    pl.semaphore_wait(bar, len(peers))

    for k in z_order:
        send(ws, wz.at[z], s_wz, r_wz, at(zk(k), y, c, x))
    local(ws, wz.at[z], r_wz)
    recv(va.at[:, :, pl.ds(0, 4)], loc.at[2])
    for p in PLANES:
        for d in range(nz):
            for j in range(4):
                r0 = (d * 4 + j) * 8
                fe[p, r0:r0 + 8, :] = va[p, d, j].astype(F32)
        for d in range(nz):
            et[p, d, 0:4, :] = (
                fe[p, pl.ds((d - 1) * 32 + 7, 4, stride=8), :] if d else jnp.zeros((4, 128), F32)
            )
            et[p, d, 4:8, :] = (
                fe[p, pl.ds((d + 1) * 32, 4, stride=8), :] if d < nz - 1 else jnp.zeros((4, 128), F32)
            )
            va[p, d, 4] = et[p, d].astype(BF16)
        for k in z_order:
            d = zk(k)
            send(
                *(va.at[p, d], rz.at[p, z], s_vz, r_vz.at[p], at(d, y, c, x))
            )
        local(va.at[p, z], rz.at[p, z], r_vz.at[p])

    recv(wz, r_wz)
    yoff = pl.multiple_of(y * blk, blk)

    def arrange(t):
        for s in range(nz):
            wf[t, 4 * s:4 * s + 4, :] = wz[s, t].astype(F32)
        wt[x, t, pl.ds(yoff, blk), :] = jnp.dot(
            wf[t].astype(BF16), perm, preferred_element_type=F32
        ).astype(BF16)

    def rows(yy):
        return pl.ds(pl.multiple_of(yy * blk, blk), blk)

    def part_rows(yy, h):
        if h is None:
            return rows(yy)
        return pl.ds(pl.multiple_of(yy * blk + h * (blk // 2), blk // 2), blk // 2)

    def w1(g, yy, h=None):
        return wt.at[g, pl.ds(0, N1), part_rows(yy, h), :]

    def w2(g, yy, h=None):
        return wt.at[g, pl.ds(N1, 7 - N1), part_rows(yy, h), :]

    def w3(yy):
        return wt.at[x, 7, rows(yy), pl.ds(0, min(128, n_in))]

    def xk(k):
        return lax.rem(x + k + NXT, NXT)

    for t in range(N1):
        arrange(t)
    for k in (1, 3, 2):
        send(w1(x, y), w1(x, y), s_wa, r_wa.at[0, k - 1], at(z, yk(k), c, x))
    for t in range(N1, 8):
        arrange(t)
    for k in (1, 3, 2):
        send(w2(x, y), w2(x, y), s_wa, r_wa.at[1, k - 1], at(z, y, c, xk(k)))
        send(w3(y), w3(y), s_w3, r_w3, at(z, yk(k), c, x))

    def forward(q):
        yq, xq = yk(-q), xk(-q)
        if q:
            recv(w1(x, yq), r_wa.at[0, q - 1])
        for k in (1, 3):
            to = at(z, y, c, xk(k))
            send(w1(x, yq), w1(x, yq), s_wb, r_wb.at[0, q, k // 2], to)
        if q:
            recv(w2(xq, y), r_wa.at[1, q - 1])
        for k in (1, 3):
            to = at(z, yk(k), c, x)
            send(w2(xq, y), w2(xq, y), s_wb, r_wb.at[1, q, k // 2], to)

    def pass_on(q):
        yq, xq = yk(-q), xk(-q)
        recv(w1(xk(-1), yq), r_wb.at[0, q, 0])
        half0 = w1(xk(-1), yq, 0)
        send(half0, half0, s_wb, r_wh, at(z, y, c, xk(1)))
        recv(w1(xk(1), yq), r_wb.at[0, q, 1])
        half1 = w1(xk(1), yq, 1)
        send(half1, half1, s_wb, r_wh, at(z, y, c, xk(-1)))
        recv(w2(xq, yk(-1)), r_wb.at[1, q, 0])
        half2 = w2(xq, yk(-1), 0)
        send(half2, half2, s_wb, r_wh, at(z, yk(1), c, x))
        recv(w2(xq, yk(1)), r_wb.at[1, q, 1])
        half3 = w2(xq, yk(1), 1)
        send(half3, half3, s_wb, r_wh, at(z, yk(-1), c, x))

    forward(0)

    def x_part(p, yy):
        return X.at[c, p + 1, :, pl.ds(pl.multiple_of(yy * blk, blk), blk), :]

    def volume_y(p):
        recv(rz.at[p], r_vz.at[p])
        for s in range(nz):
            for j in range(4):
                r0 = (s * 4 + j) * 8
                f[p, r0:r0 + 8, :] = rz[p, s, j].astype(F32)
        for s in range(nz):
            e = rz[p, s, 4].astype(F32)
            g2[p, 4 * s:4 * s + 4, :] = e[0:4]
            g2[5 + p, 4 * s:4 * s + 4, :] = e[4:8]
        xz[p, 0] = g2[p].astype(BF16)
        xz[p, 9] = g2[5 + p].astype(BF16)
        for r in range(8):
            xz[p, r + 1] = f[p, pl.ds(r, blk, stride=8), :].astype(BF16)
        for k in (2, 1, 3):
            d = yk(k)
            send(
                *(
                    xz.at[p, pl.ds(2 * d, 4)], x_part(p, y), s_xy, r_xy.at[p],
                    at(z, d, c, x),
                )
            )
        local(xz.at[p, pl.ds(2 * y, 4)], x_part(p, y), r_xy.at[p])

    def share(p):
        recv(X.at[c, p + 1], r_xy.at[p])
        if p == 4:
            @pl.when(x < NXT - 1)
            def _():
                send(X.at[c, 5], X.at[c, 0], s_xh.at[0], r_xh.at[0], right)
        if p == 0:
            @pl.when(x > 0)
            def _():
                send(X.at[c, 1], X.at[c, 6], s_xh.at[1], r_xh.at[1], left)
        send(X.at[c, p + 1], X.at[c, p + 1], s_cc, r_cc, sib)

    def halo():
        @pl.when(x > 0)
        def _():
            recv(X.at[c, 0], r_xh.at[0])
            send(X.at[c, 0], X.at[c, 0], s_xf.at[0], r_xf.at[0], sib)

        @pl.when(x < NXT - 1)
        def _():
            recv(X.at[c, 6], r_xh.at[1])
            send(X.at[c, 6], X.at[c, 6], s_xf.at[1], r_xf.at[1], sib)

    for step in STEPS:
        if step[0] == "v":
            volume_y(int(step[1]))
        elif step[0] == "f":
            forward(int(step[1]))
        elif step[0] == "g":
            pass_on(int(step[1]))
        elif step[0] == "c":
            share(int(step[1]))
        else:
            halo()

    recv(X.at[1 - c, pl.ds(1, 5)], r_cc)

    recv(wt.at[0, pl.ds(0, 7)], r_wh)
    recv(wt.at[pl.ds(0, 3), 7, rows(y), pl.ds(0, min(128, n_in))], r_w3)

    def halo_wait():
        @pl.when(x > 0)
        def _():
            recv(X.at[1 - c, 0], r_xf.at[0])

        @pl.when(x < NXT - 1)
        def _():
            recv(X.at[1 - c, 6], r_xf.at[1])

    bias = wt[x, 7].astype(F32)[:, 0:1]
    lane = lax.broadcasted_iota(jnp.int32, (half, 128), 1)

    def compute(p):
        acc = None
        for a in range(3):
            for bq in range(3):
                t = 9 * a + 3 * bq
                lhs = jnp.concatenate([wt[tap_slot(t + q)] for q in range(3)], axis=0)
                rhs = jnp.concatenate(
                    [
                        jnp.concatenate([X[0, p + a, r + bq], X[1, p + a, r + bq]], axis=0)
                        for r in range(2)
                    ],
                    axis=1,
                )
                part = jnp.dot(lhs, rhs, preferred_element_type=F32)
                acc = part if acc is None else acc + part
        for r in range(2):
            cols = acc[:, 128 * r:128 * r + 128]
            low = jnp.where(lane == 0, 0.0, pltpu.roll(cols[0:half], 1, 1))
            high = jnp.where(lane == 127, 0.0, pltpu.roll(cols[2 * half:], 127, 1))
            total = low + cols[half:2 * half] + high + bias
            O[p, r] = jnp.where(total > 0, total, 0.3 * total).astype(BF16)

    def out_y(p):
        for k in (2, 1, 3):
            d = yk(k)
            send(
                *(
                    O.at[p, :, pl.ds(pl.multiple_of(d * blk, blk), blk), :],
                    oy.at[p, pl.ds(2 * y, 2)],
                    s_oy, r_oy.at[p], at(z, d, c, x),
                )
            )
        oy[p, pl.ds(2 * y, 2)] = O[p, :, pl.ds(yoff, blk), :]

    def out_z(p):
        recv(oy.at[p, pl.ds(0, 6)], r_oy.at[p])
        for r in range(8):
            fo[p, blk * r:blk * r + blk, :] = oy[p, r].astype(F32)
        for m in range(blk):
            oz[p, m // 4, m % 4] = fo[p, pl.ds(m, 8, stride=blk), :].astype(BF16)
        for k in z_order:
            d = zk(k)
            send(
                *(oz.at[p, d], out.at[:, p, z], s_oz, r_oz, at(d, y, c, x))
            )
        local(oz.at[p, z], out.at[:, p, z], r_oz)

    def first_z(p, i):
        for r in range(2):
            fo[p, half * r:half * r + half, :] = O[p, r].astype(F32)
            for zz in range(nz):
                for yy in range(NYT):
                    r0 = half * r + blk * yy + 4 * zz
                    fz[i, zz, r, 4 * yy:4 * yy + 4, :] = fo[p, r0:r0 + 4, :]
                oz1[i, zz, r] = fz[i, zz, r].astype(BF16)
        for k in z_order:
            d = zk(k)
            send(oz1.at[i, d], iz.at[i, z], s_z1, r_z1.at[i], at(d, y, c, x))
        local(oz1.at[i, z], iz.at[i, z], r_z1.at[i])

    def then_y(i):
        recv(iz.at[i], r_z1.at[i])
        for zz in range(nz):
            for r in range(2):
                rows16 = iz[i, zz, r].astype(F32)
                r0 = (zz * 2 + r) * 4
                for yy in range(NYT):
                    fy[i, yy, r0:r0 + 4, :] = rows16[4 * yy:4 * yy + 4]
        for yy in range(NYT):
            oy1[i, yy] = fy[i, yy].astype(BF16)
        for k in (2, 1, 3):
            d = yk(k)
            send(oy1.at[i, d], iy.at[i, y], s_y1, r_y1.at[i], at(z, d, c, x))
        local(oy1.at[i, y], iy.at[i, y], r_y1.at[i])

    def finish(p, i):
        recv(iy.at[i], r_y1.at[i])
        for yy in range(NYT):
            block = iy[i, yy].astype(F32)
            for zz in range(nz):
                fl[i, zz, 8 * yy:8 * yy + 8, :] = block[8 * zz:8 * zz + 8]
        for zz in range(nz):
            for j in range(4):
                out[j, p, zz] = fl[i, zz, pl.ds(j, 8, stride=4), :].astype(BF16)

    compute(1)
    first_z(1, 0)
    compute(2)
    first_z(2, 1)
    compute(3)
    out_y(3)
    halo_wait()
    compute(0)
    out_y(0)
    compute(4)
    out_y(4)
    then_y(0)
    out_z(3)
    then_y(1)
    out_z(0)
    out_z(4)
    finish(1, 0)
    finish(2, 1)

    recv(out.at[:, pl.ds(0, 3)], r_oz)
    recv(wz.at[pl.ds(0, nz - 1)], s_wz)
    recv(rz.at[:, pl.ds(0, nz - 1)], s_vz)
    recv(wt.at[pl.ds(0, 3), pl.ds(0, 7), rows(y), :], s_wa)
    recv(wt.at[pl.ds(0, 3), 7, rows(y), pl.ds(0, min(128, n_in))], s_w3)
    recv(wt.at[pl.ds(0, 3), pl.ds(0, 7)], s_wb)
    recv(X.at[0, pl.ds(0, 5), :, pl.ds(0, 3 * blk), :], s_xy)
    recv(X.at[0, pl.ds(1, 5)], s_cc)
    recv(O.at[pl.ds(0, 3), :, pl.ds(0, 3 * blk), :], s_oy)
    recv(oz.at[pl.ds(0, 3), pl.ds(0, nz - 1)], s_oz)
    recv(oz1.at[:, pl.ds(0, nz - 1)], s_z1)
    recv(oy1.at[:, pl.ds(0, 3)], s_y1)

    @pl.when(x < NXT - 1)
    def _():
        recv(X.at[c, 5], s_xh.at[0])
        recv(X.at[c, 6], s_xf.at[1])

    @pl.when(x > 0)
    def _():
        recv(X.at[c, 1], s_xh.at[1])
        recv(X.at[c, 0], s_xf.at[0])


def shards(nz, volume, weight, channel_bias):
    blk = 4 * nz
    half = NYT * blk
    n_in = 2 * half
    v = volume.reshape(4, 5, nz, 8, 128)
    w = weight.transpose(1, 0, 2)
    b = channel_bias.reshape(1, 4)
    vm = pltpu.VMEM
    dma = pltpu.SemaphoreType.DMA
    out = pl.pallas_call(
        functools.partial(kernel, nz),
        out_shape=pltpu.VMEM((4, 5, nz, 8, 128), BF16),
        in_specs=[pl.BlockSpec(memory_space=pl.ANY)] * 3,
        out_specs=pl.BlockSpec(memory_space=pltpu.VMEM),
        scratch_shapes=[
            vm((1, 4), BF16),
            vm((5, nz, 5, 8, 128), BF16),
            vm((5, blk * 8, 128), F32),
            vm((5, nz, 8, 128), F32),
            vm((5, nz, 5, 8, 128), BF16),
            vm((5, blk * 8, 128), F32),
            vm((10, blk, 128), F32),
            vm((5, 10, blk, 128), BF16),
            vm((2, 7, 4, half, 128), BF16),
            vm((8, 4, n_in), BF16),
            vm((nz, 8, 4, n_in), BF16),
            vm((8, blk, n_in), F32),
            vm((4, 8, half, n_in), BF16),
            vm((5, 2, half, 128), BF16),
            vm((5, 8, blk, 128), BF16),
            vm((5, 8 * blk, 128), F32),
            vm((5, nz, 4, 8, 128), BF16),
            vm((2, nz, 2, 16, 128), F32),
            vm((2, nz, 2, 16, 128), BF16),
            vm((2, nz, 2, 16, 128), BF16),
            vm((2, NYT, 8 * nz, 128), F32),
            vm((2, NYT, 8 * nz, 128), BF16),
            vm((2, NYT, 8 * nz, 128), BF16),
            vm((2, nz, 32, 128), F32),
            dma(()), dma((5,)), dma(()), dma(()),
            dma(()), dma((2, 3)), dma(()), dma(()), dma(()), dma((2, 4, 2)), dma(()),
            dma(()), dma((5,)), dma(()), dma(()), dma((2,)), dma((2,)), dma((2,)), dma((2,)),
            dma(()), dma((5,)), dma(()), dma(()), dma(()), dma((2,)), dma(()), dma((2,)), dma((3,)),
        ],
        compiler_params=pltpu.CompilerParams(
            collective_id=0, has_side_effects=True, vmem_limit_bytes=56 * 1024 * 1024
        ),
        cost_estimate=pl.CostEstimate(
            flops=2 * 640 * n_in * n_in * 27, bytes_accessed=2 * v.size * 2, transcendentals=0
        ),
    )(v, w, b)
    return out.reshape(volume.shape)


def solution(mesh):
    nz = mesh.shape["ch"] // (2 * NYT)
    return jax.shard_map(
        functools.partial(shards, nz),
        mesh=mesh,
        in_specs=(P("ch", "sp", None, None), P("ch", None, None), P("ch")),
        out_specs=P("ch", "sp", None, None),
        check_vma=False,
    )
```

```python
import functools

import jax
import jax.numpy as jnp
from jax import lax
from jax.experimental import pallas as pl
from jax.experimental.pallas import tpu as pltpu
from jax.sharding import PartitionSpec as P

NYT = 4
NXT = 4
PLANES = (4, 0, 1, 2, 3)
N1 = 5
STEPS = ("v4", "v0", "f1", "f3", "g0", "v1", "f2", "v2", "v3", "g1", "g3", "c4", "c0", "g2", "c1", "c2", "c3", "h")
MESH = pl.DeviceIdType.MESH
F32 = jnp.float32
BF16 = jnp.bfloat16


def tap_slot(t):
    return (t // 7, t % 7) if t <= 20 else (3, t - 20)


def kernel(
    nz, v_hbm, w_hbm, b_hbm, out,
    b, va, fe, et, rz, f, g2, xz, X, ws, wz, wf, wt, O, oy, fo, oz, fz, oz1, iz, fy, oy1, iy, fl,
    s_vz, r_vz, s_wz, r_wz, s_wa, r_wa, s_w3, r_w3, s_wb, r_wb, r_wh,
    s_xy, r_xy, s_cc, r_cc, s_xh, r_xh, s_xf, r_xf, s_oy, r_oy, s_oz, r_oz, s_z1, r_z1, s_y1, r_y1, loc,
):
    blk = 4 * nz
    half = NYT * blk
    ch = lax.axis_index("ch")
    x = lax.axis_index("sp")
    c = lax.rem(ch, 2)
    y = lax.rem(lax.div(ch, 2), NYT)
    z = lax.div(ch, 2 * NYT)

    def at(zz, yy, cc, xx):
        return {"ch": (zz * NYT + yy) * 2 + cc, "sp": xx}

    def zk(k):
        return lax.rem(z + k + nz, nz)

    def yk(k):
        return lax.rem(y + k + NYT, NYT)

    xl, xr = lax.rem(x + NXT - 1, NXT), lax.rem(x + 1, NXT)
    sib = at(z, y, 1 - c, x)
    right, left = at(z, y, c, xr), at(z, y, c, xl)

    def send(src, dst, ss, rs, to):
        cp = pltpu.make_async_remote_copy(
            src_ref=src, dst_ref=dst, send_sem=ss, recv_sem=rs, device_id=to, device_id_type=MESH
        )
        cp.start()
        return cp

    def recv(dst, sem):
        pltpu.make_async_copy(dst, dst, sem).wait()

    def local(src, dst, sem):
        cp = pltpu.make_async_copy(src, dst, sem)
        cp.start()
        return cp

    z_order = sorted(range(1, nz), key=lambda k: -min(k, nz - k))

    bar = pltpu.get_barrier_semaphore()
    peers = [at(zk(k), y, c, x) for k in range(1, nz)]
    peers += [at(z, yk(k), c, x) for k in range(1, NYT)]
    peers += [at(z, y, c, lax.rem(x + k, NXT)) for k in range(1, NXT)]
    peers += [sib]
    for p in peers:
        pl.semaphore_signal(bar, inc=1, device_id=p, device_id_type=MESH)
    start = jnp.minimum(7 * x, 20)
    loads = [
        local(w_hbm.at[pl.ds(start, 7)], ws.at[pl.ds(0, 7)], loc.at[0]),
        local(b_hbm, b, loc.at[1]),
    ]
    for j in range(4):
        local(v_hbm.at[j], va.at[:, :, j], loc.at[2])

    @pl.when(x == 0)
    def _():
        X[:, 0] = jnp.zeros_like(X[:, 0])

    @pl.when(x == NXT - 1)
    def _():
        X[:, 6] = jnp.zeros_like(X[:, 6])

    n_in = 2 * half
    i = lax.broadcasted_iota(jnp.int32, (n_in, n_in), 0)
    o = lax.broadcasted_iota(jnp.int32, (n_in, n_in), 1)
    to = ((i >> 2) & 1) * half + ((i >> 3) & 3) * blk + (i >> 5) * 4 + (i & 3)
    perm = jnp.where(to == o, 1.0, 0.0).astype(BF16)

    loads[1].wait()
    bb = jnp.broadcast_to(b[...].astype(F32), (4, 4))
    eye = lax.broadcasted_iota(jnp.int32, (4, 4), 0) == lax.broadcasted_iota(jnp.int32, (4, 4), 1)
    col = jnp.sum(jnp.where(eye, bb, 0.0), axis=1, keepdims=True)
    ws[7] = jnp.broadcast_to(col, ws.shape[1:]).astype(BF16)

    loads[0].wait()

    pl.semaphore_wait(bar, len(peers))

    for k in z_order:
        send(ws, wz.at[z], s_wz, r_wz, at(zk(k), y, c, x))
    local(ws, wz.at[z], r_wz)
    recv(va.at[:, :, pl.ds(0, 4)], loc.at[2])
    for p in PLANES:
        for d in range(nz):
            for j in range(4):
                r0 = (d * 4 + j) * 8
                fe[p, r0:r0 + 8, :] = va[p, d, j].astype(F32)
        for d in range(nz):
            et[p, d, 0:4, :] = (
                fe[p, pl.ds((d - 1) * 32 + 7, 4, stride=8), :] if d else jnp.zeros((4, 128), F32)
            )
            et[p, d, 4:8, :] = (
                fe[p, pl.ds((d + 1) * 32, 4, stride=8), :] if d < nz - 1 else jnp.zeros((4, 128), F32)
            )
            va[p, d, 4] = et[p, d].astype(BF16)
        for k in z_order:
            d = zk(k)
            send(
                *(va.at[p, d], rz.at[p, z], s_vz, r_vz.at[p], at(d, y, c, x))
            )
        local(va.at[p, z], rz.at[p, z], r_vz.at[p])

    recv(wz, r_wz)
    yoff = pl.multiple_of(y * blk, blk)

    def arrange(t):
        for s in range(nz):
            wf[t, 4 * s:4 * s + 4, :] = wz[s, t].astype(F32)
        wt[x, t, pl.ds(yoff, blk), :] = jnp.dot(
            wf[t].astype(BF16), perm, preferred_element_type=F32
        ).astype(BF16)

    def rows(yy):
        return pl.ds(pl.multiple_of(yy * blk, blk), blk)

    def part_rows(yy, h):
        if h is None:
            return rows(yy)
        return pl.ds(pl.multiple_of(yy * blk + h * (blk // 2), blk // 2), blk // 2)

    def w1(g, yy, h=None):
        return wt.at[g, pl.ds(0, N1), part_rows(yy, h), :]

    def w2(g, yy, h=None):
        return wt.at[g, pl.ds(N1, 7 - N1), part_rows(yy, h), :]

    def w3(yy):
        return wt.at[x, 7, rows(yy), pl.ds(0, min(128, n_in))]

    def xk(k):
        return lax.rem(x + k + NXT, NXT)

    for t in range(N1):
        arrange(t)
    for k in (1, 3, 2):
        send(w1(x, y), w1(x, y), s_wa, r_wa.at[0, k - 1], at(z, yk(k), c, x))
    for t in range(N1, 8):
        arrange(t)
    for k in (1, 3, 2):
        send(w2(x, y), w2(x, y), s_wa, r_wa.at[1, k - 1], at(z, y, c, xk(k)))
        send(w3(y), w3(y), s_w3, r_w3, at(z, yk(k), c, x))

    def forward(q):
        yq, xq = yk(-q), xk(-q)
        if q:
            recv(w1(x, yq), r_wa.at[0, q - 1])
        for k in (1, 3):
            to = at(z, y, c, xk(k))
            send(w1(x, yq), w1(x, yq), s_wb, r_wb.at[0, q, k // 2], to)
        if q:
            recv(w2(xq, y), r_wa.at[1, q - 1])
        for k in (1, 3):
            to = at(z, yk(k), c, x)
            send(w2(xq, y), w2(xq, y), s_wb, r_wb.at[1, q, k // 2], to)

    def pass_on(q):
        yq, xq = yk(-q), xk(-q)
        recv(w1(xk(-1), yq), r_wb.at[0, q, 0])
        half0 = w1(xk(-1), yq, 0)
        send(half0, half0, s_wb, r_wh, at(z, y, c, xk(1)))
        recv(w1(xk(1), yq), r_wb.at[0, q, 1])
        half1 = w1(xk(1), yq, 1)
        send(half1, half1, s_wb, r_wh, at(z, y, c, xk(-1)))
        recv(w2(xq, yk(-1)), r_wb.at[1, q, 0])
        half2 = w2(xq, yk(-1), 0)
        send(half2, half2, s_wb, r_wh, at(z, yk(1), c, x))
        recv(w2(xq, yk(1)), r_wb.at[1, q, 1])
        half3 = w2(xq, yk(1), 1)
        send(half3, half3, s_wb, r_wh, at(z, yk(-1), c, x))

    forward(0)

    def x_part(p, yy):
        return X.at[c, p + 1, :, pl.ds(pl.multiple_of(yy * blk, blk), blk), :]

    def volume_y(p):
        recv(rz.at[p], r_vz.at[p])
        for s in range(nz):
            for j in range(4):
                r0 = (s * 4 + j) * 8
                f[p, r0:r0 + 8, :] = rz[p, s, j].astype(F32)
        for s in range(nz):
            e = rz[p, s, 4].astype(F32)
            g2[p, 4 * s:4 * s + 4, :] = e[0:4]
            g2[5 + p, 4 * s:4 * s + 4, :] = e[4:8]
        xz[p, 0] = g2[p].astype(BF16)
        xz[p, 9] = g2[5 + p].astype(BF16)
        for r in range(8):
            xz[p, r + 1] = f[p, pl.ds(r, blk, stride=8), :].astype(BF16)
        for k in (2, 1, 3):
            d = yk(k)
            send(
                *(
                    xz.at[p, pl.ds(2 * d, 4)], x_part(p, y), s_xy, r_xy.at[p],
                    at(z, d, c, x),
                )
            )
        local(xz.at[p, pl.ds(2 * y, 4)], x_part(p, y), r_xy.at[p])

    def share(p):
        recv(X.at[c, p + 1], r_xy.at[p])
        if p == 4:
            @pl.when(x < NXT - 1)
            def _():
                send(X.at[c, 5], X.at[c, 0], s_xh.at[0], r_xh.at[0], right)
        if p == 0:
            @pl.when(x > 0)
            def _():
                send(X.at[c, 1], X.at[c, 6], s_xh.at[1], r_xh.at[1], left)
        send(X.at[c, p + 1], X.at[c, p + 1], s_cc, r_cc, sib)

    def halo():
        @pl.when(x > 0)
        def _():
            recv(X.at[c, 0], r_xh.at[0])
            send(X.at[c, 0], X.at[c, 0], s_xf.at[0], r_xf.at[0], sib)

        @pl.when(x < NXT - 1)
        def _():
            recv(X.at[c, 6], r_xh.at[1])
            send(X.at[c, 6], X.at[c, 6], s_xf.at[1], r_xf.at[1], sib)

    for step in STEPS:
        if step[0] == "v":
            volume_y(int(step[1]))
        elif step[0] == "f":
            forward(int(step[1]))
        elif step[0] == "g":
            pass_on(int(step[1]))
        elif step[0] == "c":
            share(int(step[1]))
        else:
            halo()

    recv(X.at[1 - c, pl.ds(1, 5)], r_cc)

    recv(wt.at[0, pl.ds(0, 7)], r_wh)
    recv(wt.at[pl.ds(0, 3), 7, rows(y), pl.ds(0, min(128, n_in))], r_w3)

    def halo_wait():
        @pl.when(x > 0)
        def _():
            recv(X.at[1 - c, 0], r_xf.at[0])

        @pl.when(x < NXT - 1)
        def _():
            recv(X.at[1 - c, 6], r_xf.at[1])

    bias = wt[x, 7].astype(F32)[:, 0:1]
    lane = lax.broadcasted_iota(jnp.int32, (half, 128), 1)

    def compute(p):
        acc = None
        for a in range(3):
            for bq in range(3):
                t = 9 * a + 3 * bq
                lhs = jnp.concatenate([wt[tap_slot(t + q)] for q in range(3)], axis=0)
                rhs = jnp.concatenate(
                    [
                        jnp.concatenate([X[0, p + a, r + bq], X[1, p + a, r + bq]], axis=0)
                        for r in range(2)
                    ],
                    axis=1,
                )
                part = jnp.dot(lhs, rhs, preferred_element_type=F32)
                acc = part if acc is None else acc + part
        for r in range(2):
            cols = acc[:, 128 * r:128 * r + 128]
            low = jnp.where(lane == 0, 0.0, pltpu.roll(cols[0:half], 1, 1))
            high = jnp.where(lane == 127, 0.0, pltpu.roll(cols[2 * half:], 127, 1))
            total = low + cols[half:2 * half] + high + bias
            O[p, r] = jnp.where(total > 0, total, 0.3 * total).astype(BF16)

    def out_y(p):
        for k in (2, 1, 3):
            d = yk(k)
            send(
                *(
                    O.at[p, :, pl.ds(pl.multiple_of(d * blk, blk), blk), :],
                    oy.at[p, pl.ds(2 * y, 2)],
                    s_oy, r_oy.at[p], at(z, d, c, x),
                )
            )
        oy[p, pl.ds(2 * y, 2)] = O[p, :, pl.ds(yoff, blk), :]

    def out_z(p):
        recv(oy.at[p, pl.ds(0, 6)], r_oy.at[p])
        for r in range(8):
            fo[p, blk * r:blk * r + blk, :] = oy[p, r].astype(F32)
        for m in range(blk):
            oz[p, m // 4, m % 4] = fo[p, pl.ds(m, 8, stride=blk), :].astype(BF16)
        for k in z_order:
            d = zk(k)
            send(
                *(oz.at[p, d], out.at[:, p, z], s_oz, r_oz, at(d, y, c, x))
            )
        local(oz.at[p, z], out.at[:, p, z], r_oz)

    def first_z(p, i):
        for r in range(2):
            fo[p, half * r:half * r + half, :] = O[p, r].astype(F32)
            for zz in range(nz):
                for yy in range(NYT):
                    r0 = half * r + blk * yy + 4 * zz
                    fz[i, zz, r, 4 * yy:4 * yy + 4, :] = fo[p, r0:r0 + 4, :]
                oz1[i, zz, r] = fz[i, zz, r].astype(BF16)
        for k in z_order:
            d = zk(k)
            send(oz1.at[i, d], iz.at[i, z], s_z1, r_z1.at[i], at(d, y, c, x))
        local(oz1.at[i, z], iz.at[i, z], r_z1.at[i])

    def then_y(i):
        recv(iz.at[i], r_z1.at[i])
        for zz in range(nz):
            for r in range(2):
                rows16 = iz[i, zz, r].astype(F32)
                r0 = (zz * 2 + r) * 4
                for yy in range(NYT):
                    fy[i, yy, r0:r0 + 4, :] = rows16[4 * yy:4 * yy + 4]
        for yy in range(NYT):
            oy1[i, yy] = fy[i, yy].astype(BF16)
        for k in (2, 1, 3):
            d = yk(k)
            send(oy1.at[i, d], iy.at[i, y], s_y1, r_y1.at[i], at(z, d, c, x))
        local(oy1.at[i, y], iy.at[i, y], r_y1.at[i])

    def finish(p, i):
        recv(iy.at[i], r_y1.at[i])
        for yy in range(NYT):
            block = iy[i, yy].astype(F32)
            for zz in range(nz):
                fl[i, zz, 8 * yy:8 * yy + 8, :] = block[8 * zz:8 * zz + 8]
        for zz in range(nz):
            for j in range(4):
                out[j, p, zz] = fl[i, zz, pl.ds(j, 8, stride=4), :].astype(BF16)

    compute(1)
    first_z(1, 0)
    compute(2)
    first_z(2, 1)
    compute(3)
    out_y(3)
    halo_wait()
    compute(0)
    out_y(0)
    compute(4)
    out_y(4)
    out_z(3)
    then_y(0)
    out_z(0)
    then_y(1)
    out_z(4)
    finish(1, 0)
    finish(2, 1)

    recv(out.at[:, pl.ds(0, 3)], r_oz)
    recv(wz.at[pl.ds(0, nz - 1)], s_wz)
    recv(rz.at[:, pl.ds(0, nz - 1)], s_vz)
    recv(wt.at[pl.ds(0, 3), pl.ds(0, 7), rows(y), :], s_wa)
    recv(wt.at[pl.ds(0, 3), 7, rows(y), pl.ds(0, min(128, n_in))], s_w3)
    recv(wt.at[pl.ds(0, 3), pl.ds(0, 7)], s_wb)
    recv(X.at[0, pl.ds(0, 5), :, pl.ds(0, 3 * blk), :], s_xy)
    recv(X.at[0, pl.ds(1, 5)], s_cc)
    recv(O.at[pl.ds(0, 3), :, pl.ds(0, 3 * blk), :], s_oy)
    recv(oz.at[pl.ds(0, 3), pl.ds(0, nz - 1)], s_oz)
    recv(oz1.at[:, pl.ds(0, nz - 1)], s_z1)
    recv(oy1.at[:, pl.ds(0, 3)], s_y1)

    @pl.when(x < NXT - 1)
    def _():
        recv(X.at[c, 5], s_xh.at[0])
        recv(X.at[c, 6], s_xf.at[1])

    @pl.when(x > 0)
    def _():
        recv(X.at[c, 1], s_xh.at[1])
        recv(X.at[c, 0], s_xf.at[0])


def shards(nz, volume, weight, channel_bias):
    blk = 4 * nz
    half = NYT * blk
    n_in = 2 * half
    v = volume.reshape(4, 5, nz, 8, 128)
    w = weight.transpose(1, 0, 2)
    b = channel_bias.reshape(1, 4)
    vm = pltpu.VMEM
    dma = pltpu.SemaphoreType.DMA
    out = pl.pallas_call(
        functools.partial(kernel, nz),
        out_shape=pltpu.VMEM((4, 5, nz, 8, 128), BF16),
        in_specs=[pl.BlockSpec(memory_space=pl.ANY)] * 3,
        out_specs=pl.BlockSpec(memory_space=pltpu.VMEM),
        scratch_shapes=[
            vm((1, 4), BF16),
            vm((5, nz, 5, 8, 128), BF16),
            vm((5, blk * 8, 128), F32),
            vm((5, nz, 8, 128), F32),
            vm((5, nz, 5, 8, 128), BF16),
            vm((5, blk * 8, 128), F32),
            vm((10, blk, 128), F32),
            vm((5, 10, blk, 128), BF16),
            vm((2, 7, 4, half, 128), BF16),
            vm((8, 4, n_in), BF16),
            vm((nz, 8, 4, n_in), BF16),
            vm((8, blk, n_in), F32),
            vm((4, 8, half, n_in), BF16),
            vm((5, 2, half, 128), BF16),
            vm((5, 8, blk, 128), BF16),
            vm((5, 8 * blk, 128), F32),
            vm((5, nz, 4, 8, 128), BF16),
            vm((2, nz, 2, 16, 128), F32),
            vm((2, nz, 2, 16, 128), BF16),
            vm((2, nz, 2, 16, 128), BF16),
            vm((2, NYT, 8 * nz, 128), F32),
            vm((2, NYT, 8 * nz, 128), BF16),
            vm((2, NYT, 8 * nz, 128), BF16),
            vm((2, nz, 32, 128), F32),
            dma(()), dma((5,)), dma(()), dma(()),
            dma(()), dma((2, 3)), dma(()), dma(()), dma(()), dma((2, 4, 2)), dma(()),
            dma(()), dma((5,)), dma(()), dma(()), dma((2,)), dma((2,)), dma((2,)), dma((2,)),
            dma(()), dma((5,)), dma(()), dma(()), dma(()), dma((2,)), dma(()), dma((2,)), dma((3,)),
        ],
        compiler_params=pltpu.CompilerParams(
            collective_id=0, has_side_effects=True, vmem_limit_bytes=56 * 1024 * 1024
        ),
        cost_estimate=pl.CostEstimate(
            flops=2 * 640 * n_in * n_in * 27, bytes_accessed=2 * v.size * 2, transcendentals=0
        ),
    )(v, w, b)
    return out.reshape(volume.shape)


def solution(mesh):
    nz = mesh.shape["ch"] // (2 * NYT)
    return jax.shard_map(
        functools.partial(shards, nz),
        mesh=mesh,
        in_specs=(P("ch", "sp", None, None), P("ch", None, None), P("ch")),
        out_specs=P("ch", "sp", None, None),
        check_vma=False,
    )
```
